32 devices in a mesh: chip: 16 (over z, y, x), cores: 2 (over core).
Axes of the slice: x: 2, y: 2, z: 4, core: 2. Of those that a mesh axis runs over, the one named last changes fastest.
Arguments:
- patch_field: float32 [512, 6, 128, 128], P(('chip', 'cores')), may hold values from -6 to 6
- patch_tables: float32 [512, 6, 128, 128], P(('chip', 'cores')), may hold values from -0.5 to 0.5
- coupling: float32 [512, 5, 6, 6], P(('chip', 'cores')), may hold values from -1 to 1
- side_device: int32 [4096, 1], replicated, may hold values from 0 to 31; in each aligned block of 128 rows (0 to 127, 128 to 255, ...) at most 8 rows name the same one
- side_detail: int32 [4096, 4], replicated, may hold values from 0 to 96, as said below
- penalty: float32 [2048, 2, 128], P(('chip', 'cores')), may hold values from 0.1 to 1
- angles: float32 [2048, 3], P(('chip', 'cores')), may hold values from -3.140625 to 3.140625
Outputs:
- response: float32 [512, 6, 128, 128], P(('chip', 'cores'))
The draws below stay inside these ranges and needn't reach their ends.
Inputs may be any that keep to these rules, and one draw needn't show every extreme that they name: `side_device`: in each aligned block of 128 rows (the sides of the interfaces whose quadrature one device owns) no device is named by more than 8 rows, and some device is named by exactly 8 rows. Each owner has exactly 128 sides. `side_detail`: column 0 is below 16, column 1 below 4, column 2 below 32, column 3 from 64 to 96.
All inputs are finite; a program needn't handle non-finite values.
Results may differ from the reference program's by a relative error of at most 0.0003.
Values sent between devices are 32-bit elements; how exact they have to be, the bound alone decides.
No kernel may reach another device: no remote copies, remote signals or barrier semaphores. Data moves between devices by JAX's collectives and lax.ppermute only.
A program may use at most 192 MiB of HBM per device.

```python
import math
import jax
import jax.numpy as jnp
import numpy as np
from jax import lax

NP = 128
Q = 128
P_DEV = 16
IF_DEV = 64
NPATCH = 512
IFACES = 2048
SIDES = 4096
CAP = 8
N_CHIP = 16
N_CORES = 2


def draw_side_detail(key, part):
    keys = jax.random.split(jax.random.fold_in(key, 17), 4)
    local = jax.random.randint(keys[0], (SIDES,), 0, P_DEV)
    edges = jax.random.randint(keys[1], (SIDES,), 0, 4)
    starts = jax.random.randint(keys[2], (SIDES,), 0, NP // 4)
    lengths = jax.random.randint(keys[3], (SIDES,), NP // 2, NP // 2 + NP // 4 + 1)
    return jnp.stack([local, edges, starts, lengths], axis=1).astype(jnp.int32)


def block_scale(rng, extent, cuts, smallest, top_value):
    gain = 1.0
    for axis_at, shards_of in cuts:
        steps = jax.random.uniform(jax.random.fold_in(jax.random.fold_in(rng, 6), axis_at), (shards_of,), jnp.float32, smallest / len(cuts), top_value / len(cuts))
        gain = gain * jnp.repeat(jnp.exp(steps), extent[axis_at] // shards_of).reshape((-1,) + (1,) * (len(extent) - 1 - axis_at))
    return gain


def assign_block(key, own, number, rows, count, top, reach, lean):
    sequence = jax.random.permutation(key, count)
    crowded, common = load_shares(count, rows * top, reach, lean, True), load_shares(count, rows * top, reach, lean, False)
    places = jnp.arange(count)

    def named(sizes, offset_by):
        used = int((sizes > 0).sum())
        fixed = max(1, used // 4)
        moved = fixed + (places - fixed + offset_by * (used - fixed)) % max(1, count - fixed)
        return jnp.zeros((count,), jnp.int32).at[sequence[jnp.where(places < fixed, places, moved)]].set(jnp.asarray(sizes, jnp.int32))

    sizes = jnp.where(number % 4 == 0, named(crowded, number // 4), named(common, number - number // 4 - 1))
    mixed = jax.random.permutation(jax.random.fold_in(own, 3), count)
    donor, sink = mixed[0:count // 2 * 2:2], mixed[1:count // 2 * 2:2]
    slack = jnp.minimum(sizes[donor] - 1, reach - sizes[sink]) // 2
    slack = jnp.where((donor == sequence[0]) | (sink == sequence[0]) | (sizes[sink] == 0), 0, jnp.maximum(slack, 0))
    moved = jax.random.randint(jax.random.fold_in(own, 4), (count // 2,), 0, 1 << 20) % (slack + 1)
    sizes = sizes.at[donor].add(-moved).at[sink].add(moved)
    members = jnp.searchsorted(jnp.cumsum(sizes), jnp.arange(rows * top), side="right").astype(jnp.int32)
    table = members.reshape(top, rows).T
    table = table[jax.random.permutation(jax.random.fold_in(own, 1), rows)]
    offset_by = jax.random.randint(jax.random.fold_in(own, 2), (rows, 1), 0, top)
    return jnp.take_along_axis(table, (jnp.arange(top)[None, :] + offset_by) % top, axis=1)


def load_shares(amount, total, most, slope, full):
    portions = [(1 << 20) // math.isqrt(rank ** slope) + 1 for rank in range(1, amount + 1)]
    largest = most if full else min(most, max(-(-total // amount), total * portions[0] // sum(portions)))
    least = 1 if total - largest >= amount - 1 else 0
    holding, spare = [largest] + [least] * (amount - 1), total - largest - least * (amount - 1)
    while spare > 0:
        movable = [i for i in range(1, amount) if holding[i] < largest] or [i for i in range(1, amount) if holding[i] < most]
        mass, remaining = sum([portions[i] for i in movable]), spare
        for i in movable:
            extra = min(most - holding[i], max(1, remaining * portions[i] // mass), spare)
            holding[i] = holding[i] + extra
            spare = spare - extra
    return np.array(holding)


def normal_values(rng, extent, spread, reach, cuts=(), kind=jnp.bfloat16):
    level = block_scale(rng, extent, cuts, -0.22, 0.18) if cuts else 1.0
    drawn = jax.random.normal(rng, extent, jnp.float32) * spread * level
    return jnp.minimum(jnp.maximum(drawn, -reach), reach).astype(kind)


def setup_inputs(seed: int = 0) -> dict:
    splits = jax.random.split(jax.random.key(seed), 8)
    patch_field = normal_values(splits[0], (NPATCH, 6, NP, NP), 1.0, 6.0, ((0, 32),), jnp.float32)
    patch_tables = normal_values(splits[1], (NPATCH, 6, NP, NP), NP ** -0.5, 0.5, ((0, 32),), jnp.float32)
    coupling = normal_values(splits[2], (NPATCH, 5, 6, 6), 30 ** -0.5, 1.0, ((0, 32),), jnp.float32)
    side_device_keys = jax.random.split(jax.random.fold_in(splits[3], 1), SIDES // (2 * IF_DEV))
    side_device_turns = jax.random.permutation(jax.random.fold_in(splits[3], 3), SIDES // (2 * IF_DEV))
    side_device = jax.vmap(lambda own, number: assign_block(jax.random.fold_in(splits[3], 2), own, number, 2 * IF_DEV, N_CHIP * N_CORES, 1, CAP, 2))(side_device_keys, side_device_turns).reshape((SIDES, 1))
    side_detail = draw_side_detail(jax.random.fold_in(splits[7], 71), 0)
    penalty = jnp.clip(jnp.exp(math.log(1.0) - 2.3025851 * jax.random.uniform(splits[5], (IFACES, 2, Q), jnp.float32) ** block_scale(splits[5], (IFACES, 2, Q), ((0, 32),), -0.2, 0.2)), 0.1, 1.0)
    angles = jnp.clip(jax.random.uniform(splits[6], (IFACES, 3), jnp.float32, -3.140625, 3.140625), -3.140625, 3.140625)
    return {"patch_field": patch_field, "patch_tables": patch_tables, "coupling": coupling, "side_device": side_device, "side_detail": side_detail, "penalty": penalty, "angles": angles}


HIGHEST = lax.Precision.HIGHEST


def interior_apply(field_block, table_block, coupling_block):
    def left_apply(matrix):
        return jnp.einsum('pij,pcjk->pcik', matrix, field_block, precision=HIGHEST)

    def right_apply(values, matrix):
        return jnp.einsum('pcik,plk->pcil', values, matrix, precision=HIGHEST)

    stiff_x = left_apply(table_block[:, 0])
    mass_x = left_apply(table_block[:, 1])
    slope_x = left_apply(table_block[:, 2])
    terms_all = jnp.stack([right_apply(stiff_x, table_block[:, 4]), right_apply(mass_x, table_block[:, 3]),
                           right_apply(slope_x, table_block[:, 5]), right_apply(mass_x, table_block[:, 4]),
                           right_apply(slope_x, table_block[:, 4])], axis=1)
    return jnp.einsum('ptcd,ptdij->pcij', coupling_block, terms_all, precision=HIGHEST)


def edge_strips(field_block):
    first = field_block[:, :, 0:2, :]
    second = field_block[:, :, ::-1, :][:, :, 0:2, :]
    third = jnp.swapaxes(field_block[:, :, :, 0:2], 2, 3)
    fourth = jnp.swapaxes(field_block[:, :, :, ::-1][:, :, :, 0:2], 2, 3)
    return jnp.stack([first, second, third, fourth], axis=1)


def add_edges(output, forces):
    count = output.shape[-1]
    output = output.at[:, :, 0:2, :].add(forces[:, 0])
    output = output.at[:, :, count - 2:count, :].add(forces[:, 1][:, :, ::-1, :])
    output = output.at[:, :, :, 0:2].add(jnp.swapaxes(forces[:, 2], 2, 3))
    output = output.at[:, :, :, count - 2:count].add(jnp.swapaxes(forces[:, 3], 2, 3)[:, :, :, ::-1])
    return output


def spline_weight(offset):
    magnitude = jnp.abs(offset)
    inner = 0.75 - magnitude * magnitude
    outer = 0.5 * jnp.square(jnp.maximum(1.5 - magnitude, 0.0))
    return jnp.where(magnitude < 0.5, inner, outer)


def extraction(starts, lengths, quad_count, point_count):
    quad_pos = jnp.arange(quad_count, dtype=jnp.int32).astype(jnp.float32) + 0.5
    points = jnp.arange(point_count, dtype=jnp.int32).astype(jnp.float32)
    param = starts.astype(jnp.float32)[:, None] + quad_pos[None, :] * lengths.astype(jnp.float32)[:, None] / quad_count
    return spline_weight(param[:, :, None] - points[None, None, :])


def edge_traces(basis, strip_data):
    combined = 1.5 * strip_data[:, :, 0, :] - 0.5 * strip_data[:, :, 1, :]
    return jnp.einsum('sqj,scj->scq', basis, combined, precision=HIGHEST)


def spread_back(basis, loads):
    summed = jnp.einsum('sqj,scq->scj', basis, loads, precision=HIGHEST)
    return jnp.stack([1.5 * summed, -0.5 * summed], axis=2)


def frame_maps(angle_data):
    cos_a, sin_a = jnp.cos(angle_data[:, 0]), jnp.sin(angle_data[:, 0])
    cos_b, sin_b = jnp.cos(angle_data[:, 1]), jnp.sin(angle_data[:, 1])
    cos_g, sin_g = jnp.cos(angle_data[:, 2]), jnp.sin(angle_data[:, 2])
    row_one = jnp.stack([cos_g * cos_b, cos_g * sin_b * sin_a - sin_g * cos_a, cos_g * sin_b * cos_a + sin_g * sin_a], axis=1)
    row_two = jnp.stack([sin_g * cos_b, sin_g * sin_b * sin_a + cos_g * cos_a, sin_g * sin_b * cos_a - cos_g * sin_a], axis=1)
    row_three = jnp.stack([-sin_b, cos_b * sin_a, cos_b * cos_a], axis=1)
    rotation = jnp.stack([row_one, row_two, row_three], axis=1)
    zeroes = jnp.zeros_like(rotation)
    upper = jnp.concatenate([rotation, zeroes], axis=2)
    lower = jnp.concatenate([zeroes, rotation], axis=2)
    return jnp.concatenate([upper, lower], axis=1)


def penalty_loads(trace_data, penalty_data, angle_data):
    owned = penalty_data.shape[0]
    paired = trace_data.reshape((owned, 2) + trace_data.shape[1:])
    frames = frame_maps(angle_data)
    jump_data = paired[:, 0] - jnp.einsum('icd,idq->icq', frames, paired[:, 1], precision=HIGHEST)
    weights = jnp.repeat(penalty_data, 3, axis=1)
    first_load = weights * jump_data
    second_load = -jnp.einsum('idc,idq->icq', frames, first_load, precision=HIGHEST)
    return jnp.stack([first_load, second_load], axis=1).reshape(trace_data.shape)


def reference(patch_field, patch_tables, coupling, side_device, side_detail, penalty, angles):
    blocks = NPATCH // P_DEV

    def shaped(array):
        return array.reshape((blocks, P_DEV) + array.shape[1:])

    def block_apply(parts_in):
        return interior_apply(parts_in[0], parts_in[1], parts_in[2])

    result = lax.map(block_apply, (shaped(patch_field), shaped(patch_tables), shaped(coupling))).reshape(patch_field.shape)
    strips_all = edge_strips(patch_field).reshape(NPATCH * 4, 6, 2, NP)
    owners = IFACES // IF_DEV

    def one_owner(parts_in):
        devices_in, detail_in, penalty_in, angle_in = parts_in
        strip_rows = ((devices_in * P_DEV + detail_in[:, 0]) * 4 + detail_in[:, 1]).astype(jnp.int32)
        gathered = strips_all[strip_rows]
        basis = extraction(detail_in[:, 2], detail_in[:, 3], Q, NP)
        loads = penalty_loads(edge_traces(basis, gathered), penalty_in, angle_in)
        return spread_back(basis, loads), strip_rows

    forces, strip_rows = lax.map(one_owner, (side_device.reshape(owners, 2 * IF_DEV),
                                             side_detail.reshape(owners, 2 * IF_DEV, 4),
                                             penalty.reshape(owners, IF_DEV, 2, Q),
                                             angles.reshape(owners, IF_DEV, 3)))
    edge_forces = jax.ops.segment_sum(forces.reshape(SIDES, 6, 2, NP), strip_rows.reshape(SIDES), num_segments=NPATCH * 4)
    return add_edges(result, edge_forces.reshape(NPATCH, 4, 6, 2, NP))
```

```python
import functools

import jax
import jax.numpy as jnp
from jax import lax
from jax.experimental import pallas as pl
from jax.experimental.pallas import tpu as pltpu
from jax.sharding import PartitionSpec as P

F32 = jnp.float32
BF16 = jnp.bfloat16
I32 = jnp.int32
EDGES = 4
LANES = 128
ROWS = 8
VMEM_LIMIT = 48 * 1024 * 1024


def iota(shape, axis):
    return lax.broadcasted_iota(I32, shape, axis)


def halves(values):
    high = values.astype(BF16)
    low = (values - high.astype(F32)).astype(BF16)
    return high, low


def dot(left, right):
    return lax.dot_general(left, right, (((1,), (0,)), ((), ())), preferred_element_type=F32)


def dot_nt(left, right):
    return lax.dot_general(left, right, (((1,), (1,)), ((), ())), preferred_element_type=F32)


def lane_gather(values, index):
    return jnp.take_along_axis(values, index, axis=1)


class Codes:
    def __init__(self, per_device, points):
        self.bits = (points - 1).bit_length()
        self.local_bits = max(1, (per_device - 1).bit_length())
        self.mask = (1 << self.bits) - 1
        self.at_start = self.bits
        self.at_edge = 2 * self.bits
        self.at_local = self.at_edge + 2
        self.at_device = self.at_local + self.local_bits

    def pack(self, device, detail):
        return (
            (device << self.at_device)
            | (detail[..., 0] << self.at_local)
            | (detail[..., 1] << self.at_edge)
            | (detail[..., 2] << self.at_start)
            | detail[..., 3]
        )

    def length(self, code):
        return code & self.mask

    def start(self, code):
        return (code >> self.at_start) & self.mask

    def edge(self, code):
        return (code >> self.at_edge) & 3

    def local(self, code):
        return (code >> self.at_local) & ((1 << self.local_bits) - 1)

    def device(self, code):
        return code >> self.at_device


def slot_tables(fields, code, me, capacity, per_device):
    owners, _, sides = code.shape
    slots = owners * capacity
    spread = jnp.broadcast_to(code, (owners, capacity, sides)).reshape(slots, sides)
    mine = fields.device(spread) == me
    earlier = (iota((sides, sides), 0) < iota((sides, sides), 1)).astype(F32).astype(BF16)
    rank = dot(mine.astype(F32).astype(BF16), earlier).astype(I32)
    wanted = iota((slots, sides), 0) % capacity
    row = fields.edge(spread) * per_device + fields.local(spread) + 1
    value = (fields.start(spread) << 16) | row
    chosen = jnp.where(mine & (rank == wanted), value.astype(F32), 0.0)
    found = jnp.sum(chosen, axis=1, keepdims=True).astype(I32)
    return (found & 0xFFFF) - 1, found >> 16


def fold_window(tiles, last_pieces, window):
    lane = iota(tiles[0].shape, 1)
    out = []
    for at in range(5):
        if at < 4:
            out.append(jnp.where(lane < window, tiles[at], last_pieces[at]))
        else:
            out.append(tiles[at])
    return out


def unfold_last(tiles, window):
    quarter = window // 4
    lane = iota(tiles[0].shape, 1)
    lanes = tiles[0].shape[1]
    value = None
    for at in range(4):
        shift = (lanes - (window - quarter * at)) % lanes
        piece = pltpu.roll(tiles[at], shift, 1)
        value = piece if value is None else jnp.where(lane >= quarter * at, piece, value)
    return value


def pack_kernel(cfg, me_ref, code_ref, field_ref, out_ref, strips_ref):
    fields, per_device, capacity, window, batch, points = cfg
    step = pl.program_id(0)
    lane = iota((16, points), 1)
    sub = iota((16, points), 0)
    first = jnp.where(lane == 0, 1.5, jnp.where(lane == 1, -0.5, 0.0))
    second = jnp.where(lane == points - 1, 1.5, jnp.where(lane == points - 2, -0.5, 0.0))
    select = jnp.where(sub == 0, first, jnp.where(sub == 1, second, 0.0)).astype(BF16)
    select = jnp.concatenate([select, select], axis=1)
    for b in range(batch):
        patch = step * batch + b
        block = field_ref[b].reshape(6 * points, points)
        high, low = halves(block)
        columns = dot_nt(select, jnp.concatenate([high, low], axis=1))
        top = [1.5 * field_ref[b, c, 0:1, :] - 0.5 * field_ref[b, c, 1:2, :] for c in range(6)]
        bottom = [
            1.5 * field_ref[b, c, points - 1 : points, :]
            - 0.5 * field_ref[b, c, points - 2 : points - 1, :]
            for c in range(6)
        ]
        for c in range(6):
            cols = slice(c * points, (c + 1) * points)
            strips_ref[c, pl.ds(patch, 1), :] = top[c]
            strips_ref[c, pl.ds(per_device + patch, 1), :] = bottom[c]
            strips_ref[c, pl.ds(2 * per_device + patch, 1), :] = columns[0:1, cols]
            strips_ref[c, pl.ds(3 * per_device + patch, 1), :] = columns[1:2, cols]

    @pl.when(step == pl.num_programs(0) - 1)
    def _():
        edges = EDGES * per_device
        row, start = slot_tables(fields, code_ref[...], me_ref[0], capacity, per_device)
        slots = row.shape[0]
        owners = slots // capacity
        picker = jnp.where(iota((slots, 2 * edges), 1) % edges == row, 1.0, 0.0).astype(BF16)
        high, low = halves(jnp.concatenate([strips_ref[c] for c in range(6)], axis=1))
        picked = dot(picker, jnp.concatenate([high, low], axis=0))
        base = iota((slots, points), 1) + start - 1
        quarter = window // 4
        tiles = [
            lane_gather(picked[:, c * points : (c + 1) * points], base & (points - 1))
            for c in range(5)
        ]
        last = picked[:, 5 * points :]
        pieces = [
            lane_gather(last, (base - (window - quarter * at)) & (points - 1)) for at in range(4)
        ]
        for at, tile in enumerate(fold_window(tiles, pieces, window)):
            out_ref[:, at * capacity : (at + 1) * capacity, :] = tile.reshape(
                owners, capacity, points
            )


def read_slots(ref, capacity, window):
    owners, rows, lanes = ref.shape
    tiles = [
        ref[:, at * capacity : (at + 1) * capacity, :].reshape(owners * capacity, lanes)
        for at in range(5)
    ]
    tiles.append(unfold_last(tiles, window))
    return tiles


def spline_weight(offset):
    magnitude = jnp.abs(offset)
    inner = 0.75 - magnitude * magnitude
    outer = 0.5 * jnp.square(jnp.maximum(1.5 - magnitude, 0.0))
    return jnp.where(magnitude < 0.5, inner, outer)


def owner_kernel(cfg, me_ref, code_ref, arrived_ref, penalty_ref, frame_ref, out_ref, work_ref):
    fields, per_device, capacity, window, points = cfg
    sides = code_ref.shape[2]
    owned = sides // 2
    owners = arrived_ref.shape[0]
    slots = owners * capacity
    code_row = jnp.broadcast_to(code_ref[me_ref[0]], (sides, sides))
    code = jnp.transpose(code_row)
    device, device_row = fields.device(code), fields.device(code_row)
    same = device == device_row
    sub, lane = iota((sides, sides), 0), iota((sides, sides), 1)
    rank = jnp.sum(jnp.where(same & (lane < sub), 1.0, 0.0), axis=1, keepdims=True).astype(I32)
    rank_row = jnp.sum(jnp.where(same & (sub < lane), 1.0, 0.0), axis=0, keepdims=True).astype(I32)
    slot = device[:, 0:1] * capacity + rank
    slot_row = device_row[0:1] * capacity + rank_row
    taker = jnp.where(iota((sides, 2 * slots), 1) % slots == slot, 1.0, 0.0).astype(BF16)
    giver = jnp.where(iota((slots, sides), 0) == slot_row, 1.0, 0.0).astype(BF16)

    tiles = jnp.concatenate(read_slots(arrived_ref, capacity, window), axis=1)
    high, low = halves(tiles)
    taken = dot(taker, jnp.concatenate([high, low], axis=0))

    start = fields.start(code)
    length = fields.length(code).astype(F32)
    quad = iota((sides, points), 1)
    param = (quad.astype(F32) + 0.5) * length * (1.0 / points)
    centre = (param + 0.5).astype(I32)
    offset = param - centre.astype(F32)
    before = jnp.where(start + centre >= 1, 0.5 * jnp.square(0.5 - offset), 0.0)
    middle = 0.75 - offset * offset
    after = jnp.where(start + centre + 1 < points, 0.5 * jnp.square(0.5 + offset), 0.0)
    for c in range(6):
        values = taken[:, c * points : (c + 1) * points]
        work_ref[c] = (
            before * lane_gather(values, centre)
            + middle * lane_gather(values, centre + 1)
            + after * lane_gather(values, (centre + 2) & (points - 1))
        )

    frame = [jnp.broadcast_to(frame_ref[:, e : e + 1], (owned, points)) for e in range(9)]
    for b in range(2):
        ahead = [work_ref[3 * b + c, pl.ds(0, owned, stride=2), :] for c in range(3)]
        behind = [work_ref[3 * b + c, pl.ds(1, owned, stride=2), :] for c in range(3)]
        weight = penalty_ref[b]
        loads = [
            weight
            * (
                ahead[c]
                - (
                    frame[3 * c] * behind[0]
                    + frame[3 * c + 1] * behind[1]
                    + frame[3 * c + 2] * behind[2]
                )
            )
            for c in range(3)
        ]
        for c in range(3):
            work_ref[3 * b + c, pl.ds(0, owned, stride=2), :] = loads[c]
            work_ref[3 * b + c, pl.ds(1, owned, stride=2), :] = -(
                frame[c] * loads[0] + frame[3 + c] * loads[1] + frame[6 + c] * loads[2]
            )

    point = iota((sides, points), 1)
    centre_at = (point - 1).astype(F32)
    opening = jnp.floor((centre_at - 1.5) * (float(points) / length) - 0.5).astype(I32) + 1
    place = start + point - 1
    inside = (place >= 0) & (place < points)
    forces = [jnp.zeros((sides, points), F32) for _ in range(6)]
    for m in range(6):
        at = opening + m
        weight = spline_weight((at.astype(F32) + 0.5) * length * (1.0 / points) - centre_at)
        weight = jnp.where(inside & (at >= 0) & (at < points), weight, 0.0)
        index = at & (points - 1)
        for c in range(6):
            forces[c] = forces[c] + weight * lane_gather(work_ref[c], index)
    high, low = halves(jnp.concatenate(forces, axis=1))
    given = dot(jnp.concatenate([giver, giver], axis=1), jnp.concatenate([high, low], axis=0))
    tiles = [given[:, c * points : (c + 1) * points] for c in range(5)]
    last = given[:, 5 * points :]
    quarter = window // 4
    pieces = [pltpu.roll(last, window - quarter * at, 1) for at in range(4)]
    for at, tile in enumerate(fold_window(tiles, pieces, window)):
        out_ref[:, at * capacity : (at + 1) * capacity, :] = tile.reshape(owners, capacity, points)


def interior_kernel(cfg, coupling_ref, field_ref, table_ref, *rest):
    first, points = cfg
    out_ref, applied_ref, mixed_ref = rest[-3:]
    patch = pl.program_id(0) + first
    left = table_ref[0, 0:3].reshape(3 * points, points)
    left_high, left_low = halves(left)
    field_high, field_low = [], []
    for c in range(6):
        high, low = halves(field_ref[0, c])
        field_high.append(high)
        field_low.append(low)
    field_high = jnp.concatenate(field_high, axis=1)
    field_low = jnp.concatenate(field_low, axis=1)
    applied_ref[...] = dot(
        jnp.concatenate([left_high, left_low], axis=1),
        jnp.concatenate([field_high, field_high], axis=0),
    ) + dot(left_high, field_low)

    def weight(t, c, d):
        return coupling_ref[patch, (t * 6 + c) * 6 + d]

    chunk = 16
    for at in range(points // chunk):
        sums = [[None] * 6 for _ in range(3)]

        def add(group, c, value):
            have = sums[group][c]
            sums[group][c] = value if have is None else have + value

        for d in range(6):
            stiff, mass, slope = [
                applied_ref[
                    g * points + at * chunk : g * points + (at + 1) * chunk,
                    d * points : (d + 1) * points,
                ]
                for g in range(3)
            ]
            for c in range(6):
                add(0, c, weight(0, c, d) * stiff)
                add(0, c, weight(3, c, d) * mass)
                add(0, c, weight(4, c, d) * slope)
                add(1, c, weight(1, c, d) * mass)
                add(2, c, weight(2, c, d) * slope)
        for c in range(6):
            rows = pl.ds(c * points + at * chunk, chunk)
            for g in range(3):
                high, low = halves(sums[g][c])
                mixed_ref[rows, g * points : (g + 1) * points] = high
                mixed_ref[rows, (3 + g) * points : (4 + g) * points] = low

    right = jnp.concatenate([table_ref[0, 4], table_ref[0, 3], table_ref[0, 5]], axis=1)
    right_high, right_low = halves(right)
    right = jnp.concatenate([right_high, right_low], axis=0)
    both = dot_nt(mixed_ref[...], jnp.concatenate([right, right], axis=1))
    total = both[:, :points] + both[:, points:]
    out_ref[0] = total.reshape(6, points, points)


def finish_kernel(cfg, me_ref, code_ref, arrived_ref, inner_ref, out_ref, edge_ref, turned_ref):
    fields, per_device, capacity, window, batch, points = cfg
    step = pl.program_id(0)
    edges = EDGES * per_device

    @pl.when(step == 0)
    def _():
        row, start = slot_tables(fields, code_ref[...], me_ref[0], capacity, per_device)
        slots = row.shape[0]
        picker = jnp.where(iota((slots, 2 * edges), 1) % edges == row, 1.0, 0.0)
        picker = jnp.transpose(picker)[:edges].astype(BF16)
        at = iota((slots, points), 1) - start + 1
        valid = (at >= 0) & (at < window)
        index = at & (points - 1)
        tiles = [
            jnp.where(valid, lane_gather(tile, index), 0.0)
            for tile in read_slots(arrived_ref, capacity, window)
        ]
        high, low = halves(jnp.concatenate(tiles, axis=1))
        total = dot(
            jnp.concatenate([picker, picker], axis=1), jnp.concatenate([high, low], axis=0)
        )
        for c in range(6):
            edge_ref[c] = total[:, c * points : (c + 1) * points]
            part = total[2 * per_device :, c * points : (c + 1) * points]
            high = part.astype(BF16).astype(F32)
            both = jnp.concatenate([high, part - high], axis=0)
            turned_ref[c] = jnp.transpose(both).astype(BF16)

    width = batch * points
    kk = iota((edges, width), 0)
    at = iota((edges, width), 1)
    lane = at % points
    hit = (kk % per_device) == (step * batch + at // points)
    low_edge = (kk // per_device) % 2 == 0
    near = lane == jnp.where(low_edge, 0, points - 1)
    next_to = lane == jnp.where(low_edge, 1, points - 2)
    select = jnp.where(hit & near, 1.5, jnp.where(hit & next_to, -0.5, 0.0)).astype(BF16)
    sub = iota((ROWS, points), 0)
    for c in range(6):
        add = dot(turned_ref[c], select)
        for b in range(batch):
            patch = step * batch + b
            value = inner_ref[b, c] + add[:, b * points : (b + 1) * points]
            out_ref[b, c] = value
            top = jnp.broadcast_to(edge_ref[c, pl.ds(patch, 1), :], (ROWS, points))
            bottom = jnp.broadcast_to(edge_ref[c, pl.ds(per_device + patch, 1), :], (ROWS, points))
            out_ref[b, c, 0:ROWS] = value[0:ROWS] + jnp.where(
                sub == 0, 1.5 * top, jnp.where(sub == 1, -0.5 * top, 0.0)
            )
            out_ref[b, c, points - ROWS :] = value[points - ROWS :] + jnp.where(
                sub == ROWS - 1, 1.5 * bottom, jnp.where(sub == ROWS - 2, -0.5 * bottom, 0.0)
            )


def frames(angle_data):
    cos_a, sin_a = jnp.cos(angle_data[:, 0]), jnp.sin(angle_data[:, 0])
    cos_b, sin_b = jnp.cos(angle_data[:, 1]), jnp.sin(angle_data[:, 1])
    cos_g, sin_g = jnp.cos(angle_data[:, 2]), jnp.sin(angle_data[:, 2])
    return jnp.stack(
        [
            cos_g * cos_b,
            cos_g * sin_b * sin_a - sin_g * cos_a,
            cos_g * sin_b * cos_a + sin_g * sin_a,
            sin_g * cos_b,
            sin_g * sin_b * sin_a + cos_g * cos_a,
            sin_g * sin_b * cos_a - cos_g * sin_a,
            -sin_b,
            cos_b * sin_a,
            cos_b * cos_a,
        ],
        axis=1,
    )


def exchange(payload):
    return lax.all_to_all(payload, ("chip", "cores"), split_axis=0, concat_axis=0, tiled=True)


def whole(shape):
    return pl.BlockSpec(shape, lambda *_: (0,) * len(shape))


def params():
    return pltpu.CompilerParams(vmem_limit_bytes=VMEM_LIMIT)


def shards(patch_field, patch_tables, coupling, side_device, side_detail, penalty, angles):
    devices = lax.axis_size(("chip", "cores"))
    me = lax.axis_index(("chip", "cores")).astype(I32).reshape(1)
    per_device, _, points, _ = patch_field.shape
    owned = penalty.shape[0]
    sides = 2 * owned
    capacity = -(-max(2, 2 * sides // devices) // ROWS) * ROWS
    window = 3 * points // 4 + 4
    fields = Codes(per_device, points)
    smem = pl.BlockSpec(memory_space=pltpu.SMEM)
    code = fields.pack(side_device[:, 0], side_detail).reshape(devices, 1, sides)
    payload_shape = (devices, 5 * capacity, points)
    payload = jax.ShapeDtypeStruct(payload_shape, F32)
    whole_field = jax.ShapeDtypeStruct(patch_field.shape, F32)
    coupling = coupling.reshape(per_device, -1)
    frame = frames(angles)
    weights = jnp.swapaxes(penalty, 0, 1)

    batch = 4
    outgoing = pl.pallas_call(
        functools.partial(pack_kernel, (fields, per_device, capacity, window, batch, points)),
        name="pack",
        out_shape=payload,
        grid=(per_device // batch,),
        in_specs=[
            smem,
            whole(code.shape),
            pl.BlockSpec((batch, 6, points, points), lambda i: (i, 0, 0, 0)),
        ],
        out_specs=whole(payload_shape),
        scratch_shapes=[pltpu.VMEM((6, EDGES * per_device, points), F32)],
        compiler_params=params(),
    )(me, code, patch_field)

    def interior(begin, end, into, after):
        count = end - begin
        tied = lax.optimization_barrier((coupling, after))[0]
        block = pl.BlockSpec((1, 6, points, points), lambda i: (i + begin, 0, 0, 0))
        given = [] if into is None else [into]
        return pl.pallas_call(
            functools.partial(interior_kernel, (begin, points)),
            name="interior",
            out_shape=whole_field,
            grid=(count,),
            in_specs=[smem, block, block] + [pl.BlockSpec(memory_space=pl.ANY)] * len(given),
            out_specs=block,
            scratch_shapes=[
                pltpu.VMEM((3 * points, 6 * points), F32),
                pltpu.VMEM((6 * points, 6 * points), BF16),
            ],
            input_output_aliases={3: 0} if given else {},
            compiler_params=params(),
            cost_estimate=pl.CostEstimate(
                flops=count * 6 * 6 * 6 * points**3,
                bytes_accessed=count * 18 * points * points * 4,
                transcendentals=0,
            ),
        )(tied, patch_field, patch_tables, *given)

    half = per_device // 2
    arrived = exchange(outgoing)
    inner = interior(0, half, None, outgoing)
    weights, inner = lax.optimization_barrier((weights, inner))
    back = pl.pallas_call(
        functools.partial(owner_kernel, (fields, per_device, capacity, window, points)),
        name="owner",
        out_shape=payload,
        in_specs=[smem] + [pl.BlockSpec(memory_space=pltpu.VMEM)] * 4,
        out_specs=pl.BlockSpec(memory_space=pltpu.VMEM),
        scratch_shapes=[pltpu.VMEM((6, sides, points), F32)],
        compiler_params=params(),
    )(me, code, arrived, weights, frame)
    returned = exchange(back)
    inner = interior(half, per_device, inner, back)
    batch = 4
    block = pl.BlockSpec((batch, 6, points, points), lambda i: (i, 0, 0, 0))
    return pl.pallas_call(
        functools.partial(finish_kernel, (fields, per_device, capacity, window, batch, points)),
        name="finish",
        out_shape=whole_field,
        grid=(per_device // batch,),
        in_specs=[smem, whole(code.shape), whole(payload_shape), block],
        out_specs=block,
        scratch_shapes=[
            pltpu.VMEM((6, EDGES * per_device, points), F32),
            pltpu.VMEM((6, points, EDGES * per_device), BF16),
        ],
        input_output_aliases={3: 0},
        compiler_params=params(),
    )(me, code, returned, inner)


def solution(mesh):
    return jax.shard_map(
        shards,
        mesh=mesh,
        in_specs=(
            P(("chip", "cores"), None, None, None),
            P(("chip", "cores"), None, None, None),
            P(("chip", "cores"), None, None, None),
            P(),
            P(),
            P(("chip", "cores"), None, None),
            P(("chip", "cores"), None),
        ),
        out_specs=P(("chip", "cores"), None, None, None),
        check_vma=False,
    )
```

```python
import functools

import jax
import jax.numpy as jnp
from jax import lax
from jax.experimental import pallas as pl
from jax.experimental.pallas import tpu as pltpu
from jax.sharding import PartitionSpec as P

F32 = jnp.float32
BF16 = jnp.bfloat16
I32 = jnp.int32
EDGES = 4
LANES = 128
ROWS = 8
MIB = 1024 * 1024


def iota(shape, axis):
    return lax.broadcasted_iota(I32, shape, axis)


def halves(values):
    high = values.astype(BF16)
    low = (values - high.astype(F32)).astype(BF16)
    return high, low


def dot(left, right):
    return lax.dot_general(left, right, (((1,), (0,)), ((), ())), preferred_element_type=F32)


def dot_nt(left, right):
    return lax.dot_general(left, right, (((1,), (1,)), ((), ())), preferred_element_type=F32)


def lane_gather(values, index):
    return jnp.take_along_axis(values, index, axis=1)


class Codes:
    def __init__(self, per_device, points):
        self.bits = (points - 1).bit_length()
        self.local_bits = max(1, (per_device - 1).bit_length())
        self.mask = (1 << self.bits) - 1
        self.at_start = self.bits
        self.at_edge = 2 * self.bits
        self.at_local = self.at_edge + 2
        self.at_device = self.at_local + self.local_bits

    def pack(self, device, detail):
        return (
            (device << self.at_device)
            | (detail[0] << self.at_local)
            | (detail[1] << self.at_edge)
            | (detail[2] << self.at_start)
            | detail[3]
        )

    def length(self, code):
        return code & self.mask

    def start(self, code):
        return (code >> self.at_start) & self.mask

    def edge(self, code):
        return (code >> self.at_edge) & 3

    def local(self, code):
        return (code >> self.at_local) & ((1 << self.local_bits) - 1)

    def device(self, code):
        return code >> self.at_device


def side_codes(fields, device, detail):
    return fields.pack(device, [detail[i : i + 1, :] for i in range(4)])


def edge_row(fields, code):
    return fields.local(code) * EDGES + ((EDGES - fields.edge(code)) & (EDGES - 1))


def slot_tables(fields, code, me, owners, capacity):
    sides = code.shape[1] // owners
    slots = owners * capacity
    spread = jnp.concatenate(
        [
            jnp.broadcast_to(code[:, o * sides : (o + 1) * sides], (capacity, sides))
            for o in range(owners)
        ],
        axis=0,
    )
    mine = fields.device(spread) == me
    earlier = (iota((sides, sides), 0) < iota((sides, sides), 1)).astype(F32).astype(BF16)
    rank = dot(mine.astype(F32).astype(BF16), earlier).astype(I32)
    wanted = iota((slots, sides), 0) % capacity
    value = (fields.start(spread) << 16) | (edge_row(fields, spread) + 1)
    chosen = jnp.where(mine & (rank == wanted), value.astype(F32), 0.0)
    found = jnp.sum(chosen, axis=1, keepdims=True).astype(I32)
    return (found & 0xFFFF) - 1, found >> 16


def fold_window(tiles, last_pieces, window):
    lane = iota(tiles[0].shape, 1)
    out = []
    for at in range(5):
        if at < 4:
            out.append(jnp.where(lane < window, tiles[at], last_pieces[at]))
        else:
            out.append(tiles[at])
    return out


def unfold_last(tiles, window):
    quarter = window // 4
    lane = iota(tiles[0].shape, 1)
    lanes = tiles[0].shape[1]
    value = None
    for at in range(4):
        shift = (lanes - (window - quarter * at)) % lanes
        piece = pltpu.roll(tiles[at], shift, 1)
        value = piece if value is None else jnp.where(lane >= quarter * at, piece, value)
    return value


def pack_kernel(
    cfg, me_ref, device_ref, detail_ref, field_ref, out_ref, held_ref, strips_ref, arrival
):
    fields, owners, per_device, capacity, window, batch, points = cfg
    edges = EDGES * per_device
    slots = owners * capacity
    loads = []
    for patch in range(per_device):
        loads.append(
            pltpu.make_async_copy(field_ref.at[patch], held_ref.at[patch], arrival.at[patch])
        )
        loads[-1].start()

    code = side_codes(fields, device_ref[...], detail_ref)
    row, start = slot_tables(fields, code, me_ref[0], owners, capacity)
    picker = jnp.where(iota((slots, 2 * edges), 1) % edges == row, 1.0, 0.0).astype(BF16)
    base = iota((slots, points), 1) + start - 1

    lane = iota((points, points), 1)
    rows = EDGES * batch
    sub = iota((rows, points), 0)
    for step in range(per_device // batch):
        columns = jnp.zeros((points, points), F32)
        for b in range(batch):
            patch = step * batch + b
            loads[patch].wait()
            for c in range(6):
                at = EDGES * (c * batch + b)
                moved = pltpu.roll(held_ref[patch, c], (2 + at) % points, 1)
                columns = jnp.where((lane >= at) & (lane < at + EDGES), moved, columns)
        other = jnp.where(
            lane % EDGES == 1, pltpu.roll(columns, 1, 1), pltpu.roll(columns, points - 1, 1)
        )
        turned = jnp.transpose(1.5 * columns - 0.5 * other)
        for c in range(6):
            block = turned[c * rows : (c + 1) * rows]
            for b in range(batch):
                patch = step * batch + b
                top = 1.5 * held_ref[patch, c, 0:1, :] - 0.5 * held_ref[patch, c, 1:2, :]
                bottom = (
                    1.5 * held_ref[patch, c, points - 1 : points, :]
                    - 0.5 * held_ref[patch, c, points - 2 : points - 1, :]
                )
                block = jnp.where(sub == EDGES * b, top, block)
                block = jnp.where(sub == EDGES * b + 3, bottom, block)
            strips_ref[c, step * rows : (step + 1) * rows, :] = block

    high, low = halves(jnp.concatenate([strips_ref[c] for c in range(6)], axis=1))
    picked = dot(picker, jnp.concatenate([high, low], axis=0))
    quarter = window // 4
    tiles = [
        lane_gather(picked[:, c * points : (c + 1) * points], base & (points - 1))
        for c in range(5)
    ]
    last = picked[:, 5 * points :]
    pieces = [
        lane_gather(last, (base - (window - quarter * at)) & (points - 1)) for at in range(4)
    ]
    for at, tile in enumerate(fold_window(tiles, pieces, window)):
        out_ref[:, at * capacity : (at + 1) * capacity, :] = tile.reshape(owners, capacity, points)


def read_slots(ref, capacity, window):
    owners, rows, lanes = ref.shape
    tiles = [
        ref[:, at * capacity : (at + 1) * capacity, :].reshape(owners * capacity, lanes)
        for at in range(5)
    ]
    tiles.append(unfold_last(tiles, window))
    return tiles


def tables_kernel(
    cfg,
    me_ref,
    device_ref,
    detail_ref,
    angle_ref,
    gather_ref,
    start_ref,
    taker_ref,
    giver_ref,
    centre_ref,
    near_ref,
    opening_ref,
    spread_ref,
    frame_ref,
):
    fields, owners, per_device, capacity, points = cfg
    edges = EDGES * per_device
    slots = owners * capacity
    sides = device_ref.shape[1] // owners
    owned = sides // 2
    me = me_ref[0]
    code = side_codes(fields, device_ref[...], detail_ref)
    row, start = slot_tables(fields, code, me, owners, capacity)
    picker = jnp.where(iota((slots, 2 * edges), 1) % edges == row, 1.0, 0.0)
    gather = jnp.transpose(picker)[:edges].astype(BF16)
    gather_ref[...] = jnp.concatenate([gather, gather], axis=1)
    start_ref[...] = jnp.broadcast_to(start, (slots, points))

    own = pl.ds(pl.multiple_of(me * sides, sides), sides)
    own_code = fields.pack(device_ref[:, own], [detail_ref[i : i + 1, own] for i in range(4)])
    code_row = jnp.broadcast_to(own_code, (sides, sides))
    code = jnp.transpose(code_row)
    device, device_row = fields.device(code), fields.device(code_row)
    same = device == device_row
    sub, lane = iota((sides, sides), 0), iota((sides, sides), 1)
    rank = jnp.sum(jnp.where(same & (lane < sub), 1.0, 0.0), axis=1, keepdims=True).astype(I32)
    rank_row = jnp.sum(jnp.where(same & (sub < lane), 1.0, 0.0), axis=0, keepdims=True).astype(I32)
    slot = device[:, 0:1] * capacity + rank
    slot_row = device_row[0:1] * capacity + rank_row
    taker_ref[...] = jnp.where(iota((sides, 2 * slots), 1) % slots == slot, 1.0, 0.0).astype(BF16)
    giver = jnp.where(iota((slots, sides), 0) == slot_row, 1.0, 0.0).astype(BF16)
    giver_ref[...] = jnp.concatenate([giver, giver], axis=1)

    start = fields.start(code)
    length = fields.length(code).astype(F32)
    quad = iota((sides, points), 1)
    param = (quad.astype(F32) + 0.5) * length * (1.0 / points)
    centre = (param + 0.5).astype(I32)
    offset = param - centre.astype(F32)
    centre_ref[...] = centre
    near_ref[0] = jnp.where(start + centre >= 1, 0.5 * jnp.square(0.5 - offset), 0.0)
    near_ref[1] = 0.75 - offset * offset
    near_ref[2] = jnp.where(start + centre + 1 < points, 0.5 * jnp.square(0.5 + offset), 0.0)
    opening = jnp.ceil((quad.astype(F32) - 0.5) * (float(points) / length) - 0.501).astype(I32)
    opening_ref[...] = opening
    for m in range(2):
        at = opening + m
        offset = (at.astype(F32) + 0.5) * length * (1.0 / points) - quad.astype(F32)
        inside = (at >= 0) & (at < points) & (offset >= -0.5) & (offset < 0.5)
        spread_ref[3 * m] = jnp.where(
            inside & (start + quad >= 1), 0.5 * jnp.square(0.5 - offset), 0.0
        )
        spread_ref[3 * m + 1] = jnp.where(inside, 0.75 - offset * offset, 0.0)
        spread_ref[3 * m + 2] = jnp.where(
            inside & (start + quad + 1 < points), 0.5 * jnp.square(0.5 + offset), 0.0
        )

    cosine, sine = jnp.cos(angle_ref[...]), jnp.sin(angle_ref[...])
    cos_a, cos_b, cos_g = [cosine[i : i + 1] for i in range(3)]
    sin_a, sin_b, sin_g = [sine[i : i + 1] for i in range(3)]
    entries = [
        cos_g * cos_b,
        cos_g * sin_b * sin_a - sin_g * cos_a,
        cos_g * sin_b * cos_a + sin_g * sin_a,
        sin_g * cos_b,
        sin_g * sin_b * sin_a + cos_g * cos_a,
        sin_g * sin_b * cos_a - cos_g * sin_a,
        -sin_b,
        cos_b * sin_a,
        cos_b * cos_a,
    ]
    for e, entry in enumerate(entries):
        frame_ref[e] = jnp.transpose(jnp.broadcast_to(entry, (points, owned)))


def owner_kernel(
    cfg,
    arrived_ref,
    penalty_ref,
    taker_ref,
    giver_ref,
    centre_ref,
    near_ref,
    opening_ref,
    spread_ref,
    frame_ref,
    out_ref,
    work_ref,
):
    owners, capacity, window, points = cfg
    sides = taker_ref.shape[0]
    owned = sides // 2
    tiles = jnp.concatenate(read_slots(arrived_ref, capacity, window), axis=1)
    high, low = halves(tiles)
    taken = dot(taker_ref[...], jnp.concatenate([high, low], axis=0))
    centre = centre_ref[...]
    for c in range(6):
        values = taken[:, c * points : (c + 1) * points]
        work_ref[c] = (
            near_ref[0] * lane_gather(values, centre)
            + near_ref[1] * lane_gather(values, centre + 1)
            + near_ref[2] * lane_gather(values, (centre + 2) & (points - 1))
        )

    for b in range(2):
        ahead = [work_ref[3 * b + c, pl.ds(0, owned, stride=2), :] for c in range(3)]
        behind = [work_ref[3 * b + c, pl.ds(1, owned, stride=2), :] for c in range(3)]
        weight = penalty_ref[b]
        loads = [
            weight
            * (
                ahead[c]
                - (
                    frame_ref[3 * c] * behind[0]
                    + frame_ref[3 * c + 1] * behind[1]
                    + frame_ref[3 * c + 2] * behind[2]
                )
            )
            for c in range(3)
        ]
        for c in range(3):
            work_ref[3 * b + c, pl.ds(0, owned, stride=2), :] = loads[c]
            work_ref[3 * b + c, pl.ds(1, owned, stride=2), :] = -(
                frame_ref[c] * loads[0]
                + frame_ref[3 + c] * loads[1]
                + frame_ref[6 + c] * loads[2]
            )

    opening = opening_ref[...]
    forces = []
    for c in range(6):
        loads = work_ref[c]
        one = lane_gather(loads, opening & (points - 1))
        two = lane_gather(loads, (opening + 1) & (points - 1))
        force = spread_ref[0] * one + spread_ref[3] * two
        for d in range(1, 3):
            force = force + pltpu.roll(spread_ref[d] * one + spread_ref[3 + d] * two, d, 1)
        forces.append(force)
    high, low = halves(jnp.concatenate(forces, axis=1))
    given = dot(giver_ref[...], jnp.concatenate([high, low], axis=0))
    tiles = [given[:, c * points : (c + 1) * points] for c in range(5)]
    last = given[:, 5 * points :]
    quarter = window // 4
    pieces = [pltpu.roll(last, window - quarter * at, 1) for at in range(4)]
    for at, tile in enumerate(fold_window(tiles, pieces, window)):
        out_ref[:, at * capacity : (at + 1) * capacity, :] = tile.reshape(owners, capacity, points)


def interior_patch(points, weight, field_ref, table_ref, out_ref, applied_ref, mixed_ref):
    left = table_ref[0:3].reshape(3 * points, points)
    left_high, left_low = halves(left)
    field_high, field_low = [], []
    for c in range(6):
        high, low = halves(field_ref[c])
        field_high.append(high)
        field_low.append(low)
    field_high = jnp.concatenate(field_high, axis=1)
    field_low = jnp.concatenate(field_low, axis=1)
    applied_ref[...] = dot(
        jnp.concatenate([left_high, left_low], axis=1),
        jnp.concatenate([field_high, field_high], axis=0),
    ) + dot(left_high, field_low)

    chunk = points // 2
    groups = (((0, 0), (3, 1), (4, 2)), ((1, 1),), ((2, 2),))
    for at in range(points // chunk):
        for c in range(6):
            for g, terms in enumerate(groups):
                total = None
                for t, m in terms:
                    for d in range(6):
                        value = (
                            weight(t, c, d)
                            * applied_ref[
                                m * points + at * chunk : m * points + (at + 1) * chunk,
                                d * points : (d + 1) * points,
                            ]
                        )
                        total = value if total is None else total + value
                high, low = halves(total)
                rows = slice(c * points + at * chunk, c * points + (at + 1) * chunk)
                mixed_ref[rows, g * points : (g + 1) * points] = high
                mixed_ref[rows, (3 + g) * points : (4 + g) * points] = low

    right = jnp.concatenate([table_ref[4], table_ref[3], table_ref[5]], axis=1)
    right_high, right_low = halves(right)
    right = jnp.concatenate([right_high, right_low], axis=0)
    both = dot_nt(mixed_ref[...], jnp.concatenate([right, right], axis=1))
    total = both[:, :points] + both[:, points:]
    out_ref[...] = total.reshape(6, points, points)


def interior_kernel(cfg, coupling_ref, field_ref, table_ref, out_ref, applied_ref, mixed_ref):
    first, batch, points = cfg
    for b in range(batch):
        local = pl.program_id(0) * batch + b
        patch = first + local

        def weight(t, c, d):
            return coupling_ref[patch, (t * 6 + c) * 6 + d]

        interior_patch(
            points,
            weight,
            field_ref.at[b],
            table_ref.at[b],
            out_ref.at[b],
            applied_ref.at[b],
            mixed_ref.at[b],
        )


def finish_kernel(
    cfg,
    gather_ref,
    start_ref,
    arrived_ref,
    first_ref,
    second_ref,
    out_ref,
    held_ref,
    edge_ref,
    turned_ref,
    arrival,
    leaving,
):
    per_device, capacity, window, batch, points = cfg
    edges = EDGES * per_device
    steps = per_device // batch
    half = steps // 2
    loads, stores = [], []
    for step in range(steps):
        source = first_ref if step < half else second_ref
        block = pl.ds(step % half * batch, batch)
        own = held_ref.at[pl.ds(step * batch, batch)]
        loads.append(pltpu.make_async_copy(source.at[block], own, arrival.at[step]))
        loads[-1].start()
        stores.append(
            pltpu.make_async_copy(own, out_ref.at[pl.ds(step * batch, batch)], leaving.at[step])
        )

    at = iota(start_ref.shape, 1) - start_ref[...] + 1
    valid = (at >= 0) & (at < window)
    index = at & (points - 1)
    tiles = [
        jnp.where(valid, lane_gather(tile, index), 0.0)
        for tile in read_slots(arrived_ref, capacity, window)
    ]
    high, low = halves(jnp.concatenate(tiles, axis=1))
    total = dot(gather_ref[...], jnp.concatenate([high, low], axis=0))
    for c in range(6):
        part = total[:, c * points : (c + 1) * points]
        edge_ref[c] = part
        high = part.astype(BF16).astype(F32)
        both = jnp.concatenate([high, part - high], axis=0)
        turned_ref[c * points : (c + 1) * points, :] = jnp.transpose(both).astype(BF16)

    width = batch * points
    kk = iota((2 * edges, width), 0) % edges
    at = iota((2 * edges, width), 1)
    lane = at % points
    which = kk % EDGES
    near = lane == jnp.where(which == 1, points - 1, jnp.where(which == 2, 0, -1))
    next_to = lane == jnp.where(which == 1, points - 2, jnp.where(which == 2, 1, -1))
    weight = jnp.where(near, 1.5, jnp.where(next_to, -0.5, 0.0))
    ahead = kk // EDGES - at // points
    sub = iota((ROWS, points), 0)
    for step in range(steps):
        select = jnp.where(ahead == step * batch, weight, 0.0).astype(BF16)
        add = dot(turned_ref[...], select)
        loads[step].wait()
        for b in range(batch):
            patch = step * batch + b
            for c in range(6):
                value = held_ref[patch, c]
                value = value + add[c * points : (c + 1) * points, b * points : (b + 1) * points]
                top = edge_ref[c, EDGES * patch : EDGES * patch + 1, :]
                bottom = edge_ref[c, EDGES * patch + 3 : EDGES * patch + 4, :]
                held_ref[patch, c, 0:ROWS] = value[0:ROWS] + jnp.where(
                    sub == 0, 1.5 * top, jnp.where(sub == 1, -0.5 * top, 0.0)
                )
                held_ref[patch, c, ROWS : points - ROWS] = value[ROWS : points - ROWS]
                held_ref[patch, c, points - ROWS :] = value[points - ROWS :] + jnp.where(
                    sub == ROWS - 1, 1.5 * bottom, jnp.where(sub == ROWS - 2, -0.5 * bottom, 0.0)
                )
        stores[step].start()
    for store in stores:
        store.wait()


def exchange(payload):
    return lax.all_to_all(payload, ("chip", "cores"), split_axis=0, concat_axis=0, tiled=True)


def whole(shape):
    return pl.BlockSpec(shape, lambda *_: (0,) * len(shape))


def in_hbm(value):
    return pltpu.with_memory_space_constraint(value, pltpu.HBM)


def params(mib):
    return pltpu.CompilerParams(vmem_limit_bytes=mib * MIB)


def shards(patch_field, patch_tables, coupling, side_device, side_detail, penalty, angles):
    devices = lax.axis_size(("chip", "cores"))
    me = lax.axis_index(("chip", "cores")).astype(I32).reshape(1)
    per_device, _, points, _ = patch_field.shape
    owned = penalty.shape[0]
    sides = 2 * owned
    capacity = -(-max(2, 2 * sides // devices) // ROWS) * ROWS
    slots = devices * capacity
    edges = EDGES * per_device
    window = 3 * points // 4 + 4
    fields = Codes(per_device, points)
    smem = pl.BlockSpec(memory_space=pltpu.SMEM)
    vmem = pl.BlockSpec(memory_space=pltpu.VMEM)
    patch_field, patch_tables = in_hbm(patch_field), in_hbm(patch_tables)
    device_row = side_device.reshape(1, -1)
    detail_rows = side_detail.T
    payload_shape = (devices, 5 * capacity, points)
    payload = pltpu.HBM(payload_shape, F32)
    coupling = coupling.reshape(per_device, -1)
    weights = in_hbm(jnp.swapaxes(penalty, 0, 1))

    batch = 4
    outgoing = pl.pallas_call(
        functools.partial(
            pack_kernel, (fields, devices, per_device, capacity, window, batch, points)
        ),
        name="pack",
        out_shape=payload,
        grid=(1,),
        in_specs=[
            smem,
            whole(device_row.shape),
            whole(detail_rows.shape),
            pl.BlockSpec(memory_space=pl.ANY),
        ],
        out_specs=whole(payload_shape),
        scratch_shapes=[
            pltpu.VMEM(patch_field.shape, F32),
            pltpu.VMEM((6, edges, points), F32),
            pltpu.SemaphoreType.DMA((per_device,)),
        ],
        compiler_params=params(56),
    )(me, device_row, detail_rows, patch_field)
    arrived = exchange(outgoing)

    def tied(value, after):
        return lax.optimization_barrier((value, after))[0]

    def table(shape, kind):
        return jax.ShapeDtypeStruct(shape, kind)

    tables = pl.pallas_call(
        functools.partial(tables_kernel, (fields, devices, per_device, capacity, points)),
        name="tables",
        out_shape=[
            table((edges, 2 * slots), BF16),
            table((slots, points), I32),
            table((sides, 2 * slots), BF16),
            table((slots, 2 * sides), BF16),
            table((sides, points), I32),
            table((3, sides, points), F32),
            table((sides, points), I32),
            table((6, sides, points), F32),
            table((9, owned, points), F32),
        ],
        in_specs=[smem] + [vmem] * 3,
        out_specs=[vmem] * 9,
        compiler_params=params(56),
    )(tied(me, outgoing), device_row, detail_rows, angles.T)
    tables = [in_hbm(value) for value in tables]
    gather, start_table = tables[:2]

    def interior(begin, end, after):
        count = end - begin
        step = 2
        block = pl.BlockSpec((step, 6, points, points), lambda i: (i + begin // step, 0, 0, 0))
        shape = (count,) + patch_field.shape[1:]
        return pl.pallas_call(
            functools.partial(interior_kernel, (begin, step, points)),
            name="interior",
            out_shape=pltpu.HBM(shape, F32),
            grid=(count // step,),
            in_specs=[smem, block, block],
            out_specs=pl.BlockSpec((step, 6, points, points), lambda i: (i, 0, 0, 0)),
            scratch_shapes=[
                pltpu.VMEM((step, 3 * points, 6 * points), F32),
                pltpu.VMEM((step, 6 * points, 6 * points), BF16),
            ],
            compiler_params=params(48),
            cost_estimate=pl.CostEstimate(
                flops=count * 6 * 6 * 6 * points**3,
                bytes_accessed=count * 18 * points * points * 4,
                transcendentals=0,
            ),
        )(tied(coupling, after), patch_field, patch_tables)

    half = per_device // 2
    first = interior(0, half, outgoing)
    weights = tied(weights, first)
    back = pl.pallas_call(
        functools.partial(owner_kernel, (devices, capacity, window, points)),
        name="owner",
        out_shape=payload,
        grid=(1,),
        in_specs=[whole(payload_shape), whole(weights.shape)] + [whole(t.shape) for t in tables[2:]],
        out_specs=whole(payload_shape),
        scratch_shapes=[pltpu.VMEM((6, sides, points), F32)],
        compiler_params=params(40),
    )(arrived, weights, *tables[2:])
    returned = exchange(back)
    second = interior(half, per_device, back)
    gather = tied(gather, second)

    batch = 2
    anywhere = pl.BlockSpec(memory_space=pl.ANY)
    return pl.pallas_call(
        functools.partial(finish_kernel, (per_device, capacity, window, batch, points)),
        name="finish",
        out_shape=jax.ShapeDtypeStruct(patch_field.shape, F32),
        grid=(1,),
        in_specs=[
            whole(gather.shape),
            whole(start_table.shape),
            whole(payload_shape),
            anywhere,
            anywhere,
        ],
        out_specs=anywhere,
        scratch_shapes=[
            pltpu.VMEM(patch_field.shape, F32),
            pltpu.VMEM((6, edges, points), F32),
            pltpu.VMEM((6 * points, 2 * edges), BF16),
            pltpu.SemaphoreType.DMA((per_device // batch,)),
            pltpu.SemaphoreType.DMA((per_device // batch,)),
        ],
        compiler_params=params(60),
    )(gather, start_table, returned, first, second)


def solution(mesh):
    return jax.shard_map(
        shards,
        mesh=mesh,
        in_specs=(
            P(("chip", "cores"), None, None, None),
            P(("chip", "cores"), None, None, None),
            P(("chip", "cores"), None, None, None),
            P(),
            P(),
            P(("chip", "cores"), None, None),
            P(("chip", "cores"), None),
        ),
        out_specs=P(("chip", "cores"), None, None, None),
        check_vma=False,
    )
```

```python
import functools

import jax
import jax.numpy as jnp
from jax import lax
from jax.experimental import pallas as pl
from jax.experimental.pallas import tpu as pltpu
from jax.sharding import PartitionSpec as P

F32 = jnp.float32
BF16 = jnp.bfloat16
I32 = jnp.int32
EDGES = 4
LANES = 128
ROWS = 8
MIB = 1024 * 1024


def iota(shape, axis):
    return lax.broadcasted_iota(I32, shape, axis)


def halves(values):
    high = values.astype(BF16)
    low = (values - high.astype(F32)).astype(BF16)
    return high, low


def dot(left, right):
    return lax.dot_general(left, right, (((1,), (0,)), ((), ())), preferred_element_type=F32)


def dot_nt(left, right):
    return lax.dot_general(left, right, (((1,), (1,)), ((), ())), preferred_element_type=F32)


def lane_gather(values, index):
    return jnp.take_along_axis(values, index, axis=1)


class Codes:
    def __init__(self, per_device, points):
        self.bits = (points - 1).bit_length()
        self.local_bits = max(1, (per_device - 1).bit_length())
        self.mask = (1 << self.bits) - 1
        self.at_start = self.bits
        self.at_edge = 2 * self.bits
        self.at_local = self.at_edge + 2
        self.at_device = self.at_local + self.local_bits

    def pack(self, device, detail):
        return (
            (device << self.at_device)
            | (detail[0] << self.at_local)
            | (detail[1] << self.at_edge)
            | (detail[2] << self.at_start)
            | detail[3]
        )

    def length(self, code):
        return code & self.mask

    def start(self, code):
        return (code >> self.at_start) & self.mask

    def edge(self, code):
        return (code >> self.at_edge) & 3

    def local(self, code):
        return (code >> self.at_local) & ((1 << self.local_bits) - 1)

    def device(self, code):
        return code >> self.at_device


def side_codes(fields, device, detail):
    return fields.pack(device, [detail[i : i + 1, :] for i in range(4)])


def edge_row(fields, code):
    return fields.local(code) * EDGES + ((EDGES - fields.edge(code)) & (EDGES - 1))


def slot_tables(fields, code, me, owners, capacity):
    sides = code.shape[1] // owners
    slots = owners * capacity
    spread = jnp.concatenate(
        [
            jnp.broadcast_to(code[:, o * sides : (o + 1) * sides], (capacity, sides))
            for o in range(owners)
        ],
        axis=0,
    )
    mine = fields.device(spread) == me
    earlier = (iota((sides, sides), 0) < iota((sides, sides), 1)).astype(F32).astype(BF16)
    rank = dot(mine.astype(F32).astype(BF16), earlier).astype(I32)
    wanted = iota((slots, sides), 0) % capacity
    value = (fields.start(spread) << 16) | (edge_row(fields, spread) + 1)
    chosen = jnp.where(mine & (rank == wanted), value.astype(F32), 0.0)
    found = jnp.sum(chosen, axis=1, keepdims=True).astype(I32)
    return (found & 0xFFFF) - 1, found >> 16


def fold_window(tiles, last_pieces, window):
    lane = iota(tiles[0].shape, 1)
    out = []
    for at in range(5):
        if at < 4:
            out.append(jnp.where(lane < window, tiles[at], last_pieces[at]))
        else:
            out.append(tiles[at])
    return out


def unfold_last(tiles, window):
    quarter = window // 4
    lane = iota(tiles[0].shape, 1)
    lanes = tiles[0].shape[1]
    value = None
    for at in range(4):
        shift = (lanes - (window - quarter * at)) % lanes
        piece = pltpu.roll(tiles[at], shift, 1)
        value = piece if value is None else jnp.where(lane >= quarter * at, piece, value)
    return value


def pack_kernel(
    cfg, me_ref, device_ref, detail_ref, field_ref, out_ref, held_ref, strips_ref, arrival
):
    fields, owners, per_device, capacity, window, batch, points = cfg
    edges = EDGES * per_device
    slots = owners * capacity
    loads = []
    for patch in range(per_device):
        loads.append(
            pltpu.make_async_copy(field_ref.at[patch], held_ref.at[patch], arrival.at[patch])
        )
        loads[-1].start()

    code = side_codes(fields, device_ref[...], detail_ref)
    row, start = slot_tables(fields, code, me_ref[0], owners, capacity)
    picker = jnp.where(iota((slots, 2 * edges), 1) % edges == row, 1.0, 0.0).astype(BF16)
    base = iota((slots, points), 1) + start - 1

    lane = iota((points, points), 1)
    rows = EDGES * batch
    sub = iota((rows, points), 0)
    for step in range(per_device // batch):
        columns = jnp.zeros((points, points), F32)
        for b in range(batch):
            patch = step * batch + b
            loads[patch].wait()
            for c in range(6):
                at = EDGES * (c * batch + b)
                moved = pltpu.roll(held_ref[patch, c], (2 + at) % points, 1)
                columns = jnp.where((lane >= at) & (lane < at + EDGES), moved, columns)
        other = jnp.where(
            lane % EDGES == 1, pltpu.roll(columns, 1, 1), pltpu.roll(columns, points - 1, 1)
        )
        turned = jnp.transpose(1.5 * columns - 0.5 * other)
        for c in range(6):
            block = turned[c * rows : (c + 1) * rows]
            for b in range(batch):
                patch = step * batch + b
                top = 1.5 * held_ref[patch, c, 0:1, :] - 0.5 * held_ref[patch, c, 1:2, :]
                bottom = (
                    1.5 * held_ref[patch, c, points - 1 : points, :]
                    - 0.5 * held_ref[patch, c, points - 2 : points - 1, :]
                )
                block = jnp.where(sub == EDGES * b, top, block)
                block = jnp.where(sub == EDGES * b + 3, bottom, block)
            strips_ref[c, step * rows : (step + 1) * rows, :] = block

    high, low = halves(jnp.concatenate([strips_ref[c] for c in range(6)], axis=1))
    picked = dot(picker, jnp.concatenate([high, low], axis=0))
    quarter = window // 4
    tiles = [
        lane_gather(picked[:, c * points : (c + 1) * points], base & (points - 1))
        for c in range(5)
    ]
    last = picked[:, 5 * points :]
    pieces = [
        lane_gather(last, (base - (window - quarter * at)) & (points - 1)) for at in range(4)
    ]
    for at, tile in enumerate(fold_window(tiles, pieces, window)):
        out_ref[:, at * capacity : (at + 1) * capacity, :] = tile.reshape(owners, capacity, points)


def read_slots(ref, capacity, window):
    owners, rows, lanes = ref.shape
    tiles = [
        ref[:, at * capacity : (at + 1) * capacity, :].reshape(owners * capacity, lanes)
        for at in range(5)
    ]
    tiles.append(unfold_last(tiles, window))
    return tiles


def tables_kernel(
    cfg,
    me_ref,
    device_ref,
    detail_ref,
    angle_ref,
    gather_ref,
    start_ref,
    taker_ref,
    giver_ref,
    centre_ref,
    near_ref,
    opening_ref,
    spread_ref,
    frame_ref,
):
    fields, owners, per_device, capacity, points = cfg
    edges = EDGES * per_device
    slots = owners * capacity
    sides = device_ref.shape[1] // owners
    owned = sides // 2
    me = me_ref[0]
    code = side_codes(fields, device_ref[...], detail_ref)
    row, start = slot_tables(fields, code, me, owners, capacity)
    picker = jnp.where(iota((slots, 2 * edges), 1) % edges == row, 1.0, 0.0)
    gather = jnp.transpose(picker)[:edges].astype(BF16)
    gather_ref[...] = jnp.concatenate([gather, gather], axis=1)
    start_ref[...] = jnp.broadcast_to(start, (slots, points))

    own = pl.ds(pl.multiple_of(me * sides, sides), sides)
    own_code = fields.pack(device_ref[:, own], [detail_ref[i : i + 1, own] for i in range(4)])
    code_row = jnp.broadcast_to(own_code, (sides, sides))
    code = jnp.transpose(code_row)
    device, device_row = fields.device(code), fields.device(code_row)
    same = device == device_row
    sub, lane = iota((sides, sides), 0), iota((sides, sides), 1)
    rank = jnp.sum(jnp.where(same & (lane < sub), 1.0, 0.0), axis=1, keepdims=True).astype(I32)
    rank_row = jnp.sum(jnp.where(same & (sub < lane), 1.0, 0.0), axis=0, keepdims=True).astype(I32)
    slot = device[:, 0:1] * capacity + rank
    slot_row = device_row[0:1] * capacity + rank_row
    taker_ref[...] = jnp.where(iota((sides, 2 * slots), 1) % slots == slot, 1.0, 0.0).astype(BF16)
    giver = jnp.where(iota((slots, sides), 0) == slot_row, 1.0, 0.0).astype(BF16)
    giver_ref[...] = jnp.concatenate([giver, giver], axis=1)

    start = fields.start(code)
    length = fields.length(code).astype(F32)
    quad = iota((sides, points), 1)
    param = (quad.astype(F32) + 0.5) * length * (1.0 / points)
    centre = (param + 0.5).astype(I32)
    offset = param - centre.astype(F32)
    centre_ref[...] = centre
    near_ref[0] = jnp.where(start + centre >= 1, 0.5 * jnp.square(0.5 - offset), 0.0)
    near_ref[1] = 0.75 - offset * offset
    near_ref[2] = jnp.where(start + centre + 1 < points, 0.5 * jnp.square(0.5 + offset), 0.0)
    opening = jnp.ceil((quad.astype(F32) - 0.5) * (float(points) / length) - 0.501).astype(I32)
    opening_ref[...] = opening
    for m in range(2):
        at = opening + m
        offset = (at.astype(F32) + 0.5) * length * (1.0 / points) - quad.astype(F32)
        inside = (at >= 0) & (at < points) & (offset >= -0.5) & (offset < 0.5)
        spread_ref[3 * m] = jnp.where(
            inside & (start + quad >= 1), 0.5 * jnp.square(0.5 - offset), 0.0
        )
        spread_ref[3 * m + 1] = jnp.where(inside, 0.75 - offset * offset, 0.0)
        spread_ref[3 * m + 2] = jnp.where(
            inside & (start + quad + 1 < points), 0.5 * jnp.square(0.5 + offset), 0.0
        )

    cosine, sine = jnp.cos(angle_ref[...]), jnp.sin(angle_ref[...])
    cos_a, cos_b, cos_g = [cosine[i : i + 1] for i in range(3)]
    sin_a, sin_b, sin_g = [sine[i : i + 1] for i in range(3)]
    entries = [
        cos_g * cos_b,
        cos_g * sin_b * sin_a - sin_g * cos_a,
        cos_g * sin_b * cos_a + sin_g * sin_a,
        sin_g * cos_b,
        sin_g * sin_b * sin_a + cos_g * cos_a,
        sin_g * sin_b * cos_a - cos_g * sin_a,
        -sin_b,
        cos_b * sin_a,
        cos_b * cos_a,
    ]
    for e, entry in enumerate(entries):
        frame_ref[e] = jnp.transpose(jnp.broadcast_to(entry, (points, owned)))


def owner_kernel(
    cfg,
    arrived_ref,
    penalty_ref,
    taker_ref,
    giver_ref,
    centre_ref,
    near_ref,
    opening_ref,
    spread_ref,
    frame_ref,
    out_ref,
    work_ref,
):
    owners, capacity, window, points = cfg
    sides = taker_ref.shape[0]
    owned = sides // 2
    tiles = jnp.concatenate(read_slots(arrived_ref, capacity, window), axis=1)
    high, low = halves(tiles)
    taken = dot(taker_ref[...], jnp.concatenate([high, low], axis=0))
    centre = centre_ref[...]
    for c in range(6):
        values = taken[:, c * points : (c + 1) * points]
        work_ref[c] = (
            near_ref[0] * lane_gather(values, centre)
            + near_ref[1] * lane_gather(values, centre + 1)
            + near_ref[2] * lane_gather(values, (centre + 2) & (points - 1))
        )

    for b in range(2):
        ahead = [work_ref[3 * b + c, pl.ds(0, owned, stride=2), :] for c in range(3)]
        behind = [work_ref[3 * b + c, pl.ds(1, owned, stride=2), :] for c in range(3)]
        weight = penalty_ref[b]
        loads = [
            weight
            * (
                ahead[c]
                - (
                    frame_ref[3 * c] * behind[0]
                    + frame_ref[3 * c + 1] * behind[1]
                    + frame_ref[3 * c + 2] * behind[2]
                )
            )
            for c in range(3)
        ]
        for c in range(3):
            work_ref[3 * b + c, pl.ds(0, owned, stride=2), :] = loads[c]
            work_ref[3 * b + c, pl.ds(1, owned, stride=2), :] = -(
                frame_ref[c] * loads[0]
                + frame_ref[3 + c] * loads[1]
                + frame_ref[6 + c] * loads[2]
            )

    opening = opening_ref[...]
    forces = []
    for c in range(6):
        loads = work_ref[c]
        one = lane_gather(loads, opening & (points - 1))
        two = lane_gather(loads, (opening + 1) & (points - 1))
        force = spread_ref[0] * one + spread_ref[3] * two
        for d in range(1, 3):
            force = force + pltpu.roll(spread_ref[d] * one + spread_ref[3 + d] * two, d, 1)
        forces.append(force)
    high, low = halves(jnp.concatenate(forces, axis=1))
    given = dot(giver_ref[...], jnp.concatenate([high, low], axis=0))
    tiles = [given[:, c * points : (c + 1) * points] for c in range(5)]
    last = given[:, 5 * points :]
    quarter = window // 4
    pieces = [pltpu.roll(last, window - quarter * at, 1) for at in range(4)]
    for at, tile in enumerate(fold_window(tiles, pieces, window)):
        out_ref[:, at * capacity : (at + 1) * capacity, :] = tile.reshape(owners, capacity, points)


def interior_kernel(cfg, coupling_ref, _, field_ref, table_ref, out_ref, *work):
    first, batch, points = cfg
    applied, mixed = work[:batch], work[batch:]

    def apply_left(b):
        high, low = halves(table_ref[b, 0:3].reshape(3 * points, points))
        parts = [halves(field_ref[b, c]) for c in range(6)]
        field_high = jnp.concatenate([part[0] for part in parts], axis=1)
        field_low = jnp.concatenate([part[1] for part in parts], axis=1)
        applied[b][...] = dot(
            jnp.concatenate([high, low], axis=1),
            jnp.concatenate([field_high, field_high], axis=0),
        ) + dot(high, field_low)

    def mix(b):
        patch = pl.program_id(0) * batch + b + first
        groups = (((0, 0), (3, 1), (4, 2)), ((1, 1),), ((2, 2),))
        for c in range(6):
            for g, terms in enumerate(groups):
                total = None
                for t, m in terms:
                    for d in range(6):
                        rows = slice(m * points, (m + 1) * points)
                        cols = slice(d * points, (d + 1) * points)
                        value = coupling_ref[patch, (t * 6 + c) * 6 + d] * applied[b][rows, cols]
                        total = value if total is None else total + value
                high, low = halves(total)
                rows = slice(c * points, (c + 1) * points)
                mixed[b][rows, g * points : (g + 1) * points] = high
                mixed[b][rows, (3 + g) * points : (4 + g) * points] = low

    def apply_right(b):
        high, low = halves(
            jnp.concatenate([table_ref[b, 4], table_ref[b, 3], table_ref[b, 5]], axis=1)
        )
        right = jnp.concatenate([high, low], axis=0)
        both = dot_nt(mixed[b][...], jnp.concatenate([right, right], axis=1))
        total = both[:, :points] + both[:, points:]
        out_ref[b] = total.reshape(6, points, points)

    apply_left(0)
    for b in range(batch):
        if b + 1 < batch:
            apply_left(b + 1)
        if b > 0:
            apply_right(b - 1)
        mix(b)
    apply_right(batch - 1)


def finish_kernel(
    cfg,
    gather_ref,
    start_ref,
    arrived_ref,
    first_ref,
    second_ref,
    out_ref,
    held_ref,
    edge_ref,
    turned_ref,
    arrival,
    leaving,
):
    per_device, capacity, window, batch, points = cfg
    edges = EDGES * per_device
    steps = per_device // batch
    half = steps // 2
    loads, stores = [], []
    for step in range(steps):
        source = first_ref if step < half else second_ref
        block = pl.ds(step % half * batch, batch)
        own = held_ref.at[pl.ds(step * batch, batch)]
        loads.append(pltpu.make_async_copy(source.at[block], own, arrival.at[step]))
        loads[-1].start()
        stores.append(
            pltpu.make_async_copy(own, out_ref.at[pl.ds(step * batch, batch)], leaving.at[step])
        )

    at = iota(start_ref.shape, 1) - start_ref[...] + 1
    valid = (at >= 0) & (at < window)
    index = at & (points - 1)
    tiles = [
        jnp.where(valid, lane_gather(tile, index), 0.0)
        for tile in read_slots(arrived_ref, capacity, window)
    ]
    high, low = halves(jnp.concatenate(tiles, axis=1))
    total = dot(gather_ref[...], jnp.concatenate([high, low], axis=0))
    for c in range(6):
        part = total[:, c * points : (c + 1) * points]
        edge_ref[c] = part
        high = part.astype(BF16).astype(F32)
        both = jnp.concatenate([high, part - high], axis=0)
        turned_ref[c * points : (c + 1) * points, :] = jnp.transpose(both).astype(BF16)

    width = batch * points
    kk = iota((2 * edges, width), 0) % edges
    at = iota((2 * edges, width), 1)
    lane = at % points
    which = kk % EDGES
    near = lane == jnp.where(which == 1, points - 1, jnp.where(which == 2, 0, -1))
    next_to = lane == jnp.where(which == 1, points - 2, jnp.where(which == 2, 1, -1))
    weight = jnp.where(near, 1.5, jnp.where(next_to, -0.5, 0.0))
    ahead = kk // EDGES - at // points
    sub = iota((ROWS, points), 0)
    for step in range(steps):
        select = jnp.where(ahead == step * batch, weight, 0.0).astype(BF16)
        add = dot(turned_ref[...], select)
        loads[step].wait()
        for b in range(batch):
            patch = step * batch + b
            for c in range(6):
                value = held_ref[patch, c]
                value = value + add[c * points : (c + 1) * points, b * points : (b + 1) * points]
                top = edge_ref[c, EDGES * patch : EDGES * patch + 1, :]
                bottom = edge_ref[c, EDGES * patch + 3 : EDGES * patch + 4, :]
                held_ref[patch, c, 0:ROWS] = value[0:ROWS] + jnp.where(
                    sub == 0, 1.5 * top, jnp.where(sub == 1, -0.5 * top, 0.0)
                )
                held_ref[patch, c, ROWS : points - ROWS] = value[ROWS : points - ROWS]
                held_ref[patch, c, points - ROWS :] = value[points - ROWS :] + jnp.where(
                    sub == ROWS - 1, 1.5 * bottom, jnp.where(sub == ROWS - 2, -0.5 * bottom, 0.0)
                )
        stores[step].start()
    for store in stores:
        store.wait()


def exchange(payload):
    return lax.all_to_all(payload, ("chip", "cores"), split_axis=0, concat_axis=0, tiled=True)


def whole(shape):
    return pl.BlockSpec(shape, lambda *_: (0,) * len(shape))


def in_hbm(value):
    return pltpu.with_memory_space_constraint(value, pltpu.HBM)


def params(mib):
    return pltpu.CompilerParams(vmem_limit_bytes=mib * MIB)


def shards(patch_field, patch_tables, coupling, side_device, side_detail, penalty, angles):
    devices = lax.axis_size(("chip", "cores"))
    me = lax.axis_index(("chip", "cores")).astype(I32).reshape(1)
    per_device, _, points, _ = patch_field.shape
    owned = penalty.shape[0]
    sides = 2 * owned
    capacity = -(-max(2, 2 * sides // devices) // ROWS) * ROWS
    slots = devices * capacity
    edges = EDGES * per_device
    window = 3 * points // 4 + 4
    fields = Codes(per_device, points)
    smem = pl.BlockSpec(memory_space=pltpu.SMEM)
    vmem = pl.BlockSpec(memory_space=pltpu.VMEM)
    patch_field, patch_tables = in_hbm(patch_field), in_hbm(patch_tables)
    device_row = side_device.reshape(1, -1)
    detail_rows = side_detail.T
    payload_shape = (devices, 5 * capacity, points)
    payload = pltpu.HBM(payload_shape, F32)
    coupling = coupling.reshape(per_device, -1)
    weights = in_hbm(jnp.swapaxes(penalty, 0, 1))

    batch = 4
    outgoing = pl.pallas_call(
        functools.partial(
            pack_kernel, (fields, devices, per_device, capacity, window, batch, points)
        ),
        name="pack",
        out_shape=payload,
        grid=(1,),
        in_specs=[
            smem,
            whole(device_row.shape),
            whole(detail_rows.shape),
            pl.BlockSpec(memory_space=pl.ANY),
        ],
        out_specs=whole(payload_shape),
        scratch_shapes=[
            pltpu.VMEM(patch_field.shape, F32),
            pltpu.VMEM((6, edges, points), F32),
            pltpu.SemaphoreType.DMA((per_device,)),
        ],
        compiler_params=params(56),
    )(me, device_row, detail_rows, patch_field)
    arrived = exchange(outgoing)

    def tied(value, after):
        return lax.optimization_barrier((value, after))[0]

    def table(shape, kind):
        return jax.ShapeDtypeStruct(shape, kind)

    tables = pl.pallas_call(
        functools.partial(tables_kernel, (fields, devices, per_device, capacity, points)),
        name="tables",
        out_shape=[
            table((edges, 2 * slots), BF16),
            table((slots, points), I32),
            table((sides, 2 * slots), BF16),
            table((slots, 2 * sides), BF16),
            table((sides, points), I32),
            table((3, sides, points), F32),
            table((sides, points), I32),
            table((6, sides, points), F32),
            table((9, owned, points), F32),
        ],
        in_specs=[smem] + [vmem] * 3,
        out_specs=[vmem] * 9,
        compiler_params=params(56),
    )(tied(me, outgoing), device_row, detail_rows, angles.T)
    tables = [in_hbm(value) for value in tables]
    gather, start_table = tables[:2]

    def interior(begin, end, after):
        count = end - begin
        block = pl.BlockSpec((batch, 6, points, points), lambda i: (i + begin // batch, 0, 0, 0))
        shape = (count,) + patch_field.shape[1:]
        return pl.pallas_call(
            functools.partial(interior_kernel, (begin, batch, points)),
            name="interior",
            out_shape=pltpu.HBM(shape, F32),
            grid=(count // batch,),
            in_specs=[smem, smem, block, block],
            out_specs=pl.BlockSpec((batch, 6, points, points), lambda i: (i, 0, 0, 0)),
            scratch_shapes=[pltpu.VMEM((3 * points, 6 * points), F32)] * batch
            + [pltpu.VMEM((6 * points, 6 * points), BF16)] * batch,
            compiler_params=params(52),
            cost_estimate=pl.CostEstimate(
                flops=count * 6 * 6 * 6 * points**3,
                bytes_accessed=count * 18 * points * points * 4,
                transcendentals=0,
            ),
        )(coupling, tied(me, after), patch_field, patch_tables)

    half = per_device // 2
    first = in_hbm(interior(0, half, outgoing))
    weights = tied(weights, first)
    back = pl.pallas_call(
        functools.partial(owner_kernel, (devices, capacity, window, points)),
        name="owner",
        out_shape=payload,
        grid=(1,),
        in_specs=[whole(payload_shape), whole(weights.shape)] + [whole(t.shape) for t in tables[2:]],
        out_specs=whole(payload_shape),
        scratch_shapes=[pltpu.VMEM((6, sides, points), F32)],
        compiler_params=params(40),
    )(arrived, weights, *tables[2:])
    returned = exchange(back)
    second = in_hbm(interior(half, per_device, back))
    gather = tied(gather, second)

    batch = 2
    anywhere = pl.BlockSpec(memory_space=pl.ANY)
    return pl.pallas_call(
        functools.partial(finish_kernel, (per_device, capacity, window, batch, points)),
        name="finish",
        out_shape=jax.ShapeDtypeStruct(patch_field.shape, F32),
        grid=(1,),
        in_specs=[
            whole(gather.shape),
            whole(start_table.shape),
            whole(payload_shape),
            anywhere,
            anywhere,
        ],
        out_specs=anywhere,
        scratch_shapes=[
            pltpu.VMEM(patch_field.shape, F32),
            pltpu.VMEM((6, edges, points), F32),
            pltpu.VMEM((6 * points, 2 * edges), BF16),
            pltpu.SemaphoreType.DMA((per_device // batch,)),
            pltpu.SemaphoreType.DMA((per_device // batch,)),
        ],
        compiler_params=params(40),
    )(gather, start_table, returned, first, second)


def solution(mesh):
    return jax.shard_map(
        shards,
        mesh=mesh,
        in_specs=(
            P(("chip", "cores"), None, None, None),
            P(("chip", "cores"), None, None, None),
            P(("chip", "cores"), None, None, None),
            P(),
            P(),
            P(("chip", "cores"), None, None),
            P(("chip", "cores"), None),
        ),
        out_specs=P(("chip", "cores"), None, None, None),
        check_vma=False,
    )
```

```python
import functools

import jax
import jax.numpy as jnp
from jax import lax
from jax.experimental import pallas as pl
from jax.experimental.pallas import tpu as pltpu
from jax.sharding import PartitionSpec as P

F32 = jnp.float32
BF16 = jnp.bfloat16
I32 = jnp.int32
EDGES = 4
LANES = 128
ROWS = 8
MIB = 1024 * 1024


def iota(shape, axis):
    return lax.broadcasted_iota(I32, shape, axis)


def halves(values):
    high = values.astype(BF16)
    low = (values - high.astype(F32)).astype(BF16)
    return high, low


def dot(left, right):
    return lax.dot_general(left, right, (((1,), (0,)), ((), ())), preferred_element_type=F32)


def dot_nt(left, right):
    return lax.dot_general(left, right, (((1,), (1,)), ((), ())), preferred_element_type=F32)


def lane_gather(values, index):
    return jnp.take_along_axis(values, index, axis=1)


class Codes:
    def __init__(self, per_device, points):
        self.bits = (points - 1).bit_length()
        self.local_bits = max(1, (per_device - 1).bit_length())
        self.mask = (1 << self.bits) - 1
        self.at_start = self.bits
        self.at_edge = 2 * self.bits
        self.at_local = self.at_edge + 2
        self.at_device = self.at_local + self.local_bits

    def pack(self, device, detail):
        return (
            (device << self.at_device)
            | (detail[0] << self.at_local)
            | (detail[1] << self.at_edge)
            | (detail[2] << self.at_start)
            | detail[3]
        )

    def length(self, code):
        return code & self.mask

    def start(self, code):
        return (code >> self.at_start) & self.mask

    def edge(self, code):
        return (code >> self.at_edge) & 3

    def local(self, code):
        return (code >> self.at_local) & ((1 << self.local_bits) - 1)

    def device(self, code):
        return code >> self.at_device


def side_codes(fields, device, detail):
    return fields.pack(device, [detail[i : i + 1, :] for i in range(4)])


def edge_row(fields, code):
    return fields.local(code) * EDGES + ((EDGES - fields.edge(code)) & (EDGES - 1))


def slot_tables(fields, code, me, owners, capacity):
    sides = code.shape[1] // owners
    slots = owners * capacity
    spread = jnp.concatenate(
        [
            jnp.broadcast_to(code[:, o * sides : (o + 1) * sides], (capacity, sides))
            for o in range(owners)
        ],
        axis=0,
    )
    mine = fields.device(spread) == me
    earlier = (iota((sides, sides), 0) < iota((sides, sides), 1)).astype(F32).astype(BF16)
    rank = dot(mine.astype(F32).astype(BF16), earlier).astype(I32)
    wanted = iota((slots, sides), 0) % capacity
    value = (fields.start(spread) << 16) | (edge_row(fields, spread) + 1)
    chosen = jnp.where(mine & (rank == wanted), value.astype(F32), 0.0)
    found = jnp.sum(chosen, axis=1, keepdims=True).astype(I32)
    return (found & 0xFFFF) - 1, found >> 16


def fold_window(tiles, last_pieces, window):
    lane = iota(tiles[0].shape, 1)
    out = []
    for at in range(5):
        if at < 4:
            out.append(jnp.where(lane < window, tiles[at], last_pieces[at]))
        else:
            out.append(tiles[at])
    return out


def unfold_last(tiles, window):
    quarter = window // 4
    lane = iota(tiles[0].shape, 1)
    lanes = tiles[0].shape[1]
    value = None
    for at in range(4):
        shift = (lanes - (window - quarter * at)) % lanes
        piece = pltpu.roll(tiles[at], shift, 1)
        value = piece if value is None else jnp.where(lane >= quarter * at, piece, value)
    return value


def pack_kernel(
    cfg, me_ref, device_ref, detail_ref, field_ref, out_ref, held_ref, strips_ref, arrival
):
    fields, owners, per_device, capacity, window, batch, points = cfg
    edges = EDGES * per_device
    slots = owners * capacity
    loads = []
    for patch in range(per_device):
        loads.append(
            pltpu.make_async_copy(field_ref.at[patch], held_ref.at[patch], arrival.at[patch])
        )
        loads[-1].start()

    code = side_codes(fields, device_ref[...], detail_ref)
    row, start = slot_tables(fields, code, me_ref[0], owners, capacity)
    picker = jnp.where(iota((slots, 2 * edges), 1) % edges == row, 1.0, 0.0).astype(BF16)
    base = iota((slots, points), 1) + start - 1

    lane = iota((points, points), 1)
    rows = EDGES * batch
    sub = iota((rows, points), 0)
    for step in range(per_device // batch):
        columns = jnp.zeros((points, points), F32)
        for b in range(batch):
            patch = step * batch + b
            loads[patch].wait()
            for c in range(6):
                at = EDGES * (c * batch + b)
                moved = pltpu.roll(held_ref[patch, c], (2 + at) % points, 1)
                columns = jnp.where((lane >= at) & (lane < at + EDGES), moved, columns)
        other = jnp.where(
            lane % EDGES == 1, pltpu.roll(columns, 1, 1), pltpu.roll(columns, points - 1, 1)
        )
        turned = jnp.transpose(1.5 * columns - 0.5 * other)
        for c in range(6):
            block = turned[c * rows : (c + 1) * rows]
            for b in range(batch):
                patch = step * batch + b
                top = 1.5 * held_ref[patch, c, 0:1, :] - 0.5 * held_ref[patch, c, 1:2, :]
                bottom = (
                    1.5 * held_ref[patch, c, points - 1 : points, :]
                    - 0.5 * held_ref[patch, c, points - 2 : points - 1, :]
                )
                block = jnp.where(sub == EDGES * b, top, block)
                block = jnp.where(sub == EDGES * b + 3, bottom, block)
            strips_ref[c, step * rows : (step + 1) * rows, :] = block

    high, low = halves(jnp.concatenate([strips_ref[c] for c in range(6)], axis=1))
    picked = dot(picker, jnp.concatenate([high, low], axis=0))
    quarter = window // 4
    tiles = [
        lane_gather(picked[:, c * points : (c + 1) * points], base & (points - 1))
        for c in range(5)
    ]
    last = picked[:, 5 * points :]
    pieces = [
        lane_gather(last, (base - (window - quarter * at)) & (points - 1)) for at in range(4)
    ]
    for at, tile in enumerate(fold_window(tiles, pieces, window)):
        out_ref[:, at * capacity : (at + 1) * capacity, :] = tile.reshape(owners, capacity, points)


def read_slots(ref, capacity, window):
    owners, rows, lanes = ref.shape
    tiles = [
        ref[:, at * capacity : (at + 1) * capacity, :].reshape(owners * capacity, lanes)
        for at in range(5)
    ]
    tiles.append(unfold_last(tiles, window))
    return tiles


def tables_kernel(
    cfg,
    me_ref,
    device_ref,
    detail_ref,
    angle_ref,
    gather_ref,
    start_ref,
    taker_ref,
    giver_ref,
    centre_ref,
    near_ref,
    opening_ref,
    spread_ref,
    frame_ref,
):
    fields, owners, per_device, capacity, points = cfg
    edges = EDGES * per_device
    slots = owners * capacity
    sides = device_ref.shape[1] // owners
    owned = sides // 2
    me = me_ref[0]
    code = side_codes(fields, device_ref[...], detail_ref)
    row, start = slot_tables(fields, code, me, owners, capacity)
    picker = jnp.where(iota((slots, 2 * edges), 1) % edges == row, 1.0, 0.0)
    gather = jnp.transpose(picker)[:edges].astype(BF16)
    gather_ref[...] = jnp.concatenate([gather, gather], axis=1)
    start_ref[...] = jnp.broadcast_to(start, (slots, points))

    own = pl.ds(pl.multiple_of(me * sides, sides), sides)
    own_code = fields.pack(device_ref[:, own], [detail_ref[i : i + 1, own] for i in range(4)])
    code_row = jnp.broadcast_to(own_code, (sides, sides))
    code = jnp.transpose(code_row)
    device, device_row = fields.device(code), fields.device(code_row)
    same = device == device_row
    sub, lane = iota((sides, sides), 0), iota((sides, sides), 1)
    rank = jnp.sum(jnp.where(same & (lane < sub), 1.0, 0.0), axis=1, keepdims=True).astype(I32)
    rank_row = jnp.sum(jnp.where(same & (sub < lane), 1.0, 0.0), axis=0, keepdims=True).astype(I32)
    slot = device[:, 0:1] * capacity + rank
    slot_row = device_row[0:1] * capacity + rank_row
    taker_ref[...] = jnp.where(iota((sides, 2 * slots), 1) % slots == slot, 1.0, 0.0).astype(BF16)
    giver = jnp.where(iota((slots, sides), 0) == slot_row, 1.0, 0.0).astype(BF16)
    giver_ref[...] = jnp.concatenate([giver, giver], axis=1)

    start = fields.start(code)
    length = fields.length(code).astype(F32)
    quad = iota((sides, points), 1)
    param = (quad.astype(F32) + 0.5) * length * (1.0 / points)
    centre = (param + 0.5).astype(I32)
    offset = param - centre.astype(F32)
    centre_ref[...] = centre
    near_ref[0] = jnp.where(start + centre >= 1, 0.5 * jnp.square(0.5 - offset), 0.0)
    near_ref[1] = 0.75 - offset * offset
    near_ref[2] = jnp.where(start + centre + 1 < points, 0.5 * jnp.square(0.5 + offset), 0.0)
    opening = jnp.ceil((quad.astype(F32) - 0.5) * (float(points) / length) - 0.501).astype(I32)
    opening_ref[...] = opening
    for m in range(2):
        at = opening + m
        offset = (at.astype(F32) + 0.5) * length * (1.0 / points) - quad.astype(F32)
        inside = (at >= 0) & (at < points) & (offset >= -0.5) & (offset < 0.5)
        spread_ref[3 * m] = jnp.where(
            inside & (start + quad >= 1), 0.5 * jnp.square(0.5 - offset), 0.0
        )
        spread_ref[3 * m + 1] = jnp.where(inside, 0.75 - offset * offset, 0.0)
        spread_ref[3 * m + 2] = jnp.where(
            inside & (start + quad + 1 < points), 0.5 * jnp.square(0.5 + offset), 0.0
        )

    cosine, sine = jnp.cos(angle_ref[...]), jnp.sin(angle_ref[...])
    cos_a, cos_b, cos_g = [cosine[i : i + 1] for i in range(3)]
    sin_a, sin_b, sin_g = [sine[i : i + 1] for i in range(3)]
    entries = [
        cos_g * cos_b,
        cos_g * sin_b * sin_a - sin_g * cos_a,
        cos_g * sin_b * cos_a + sin_g * sin_a,
        sin_g * cos_b,
        sin_g * sin_b * sin_a + cos_g * cos_a,
        sin_g * sin_b * cos_a - cos_g * sin_a,
        -sin_b,
        cos_b * sin_a,
        cos_b * cos_a,
    ]
    for e, entry in enumerate(entries):
        frame_ref[e] = jnp.transpose(jnp.broadcast_to(entry, (points, owned)))


def owner_kernel(
    cfg,
    arrived_ref,
    penalty_ref,
    taker_ref,
    giver_ref,
    centre_ref,
    near_ref,
    opening_ref,
    spread_ref,
    frame_ref,
    out_ref,
    work_ref,
    *held,
):
    owners, capacity, window, points = cfg
    arrival = held[-1]
    tables = {}
    names = ("taker", "centre", "near", "penalty", "frame", "opening", "spread", "giver")
    sources = (
        taker_ref,
        centre_ref,
        near_ref,
        penalty_ref,
        frame_ref,
        opening_ref,
        spread_ref,
        giver_ref,
    )
    for at, (name, source) in enumerate(zip(names, sources)):
        tables[name] = (pltpu.make_async_copy(source, held[at], arrival.at[at]), held[at])
        tables[name][0].start()

    def ready(name):
        tables[name][0].wait()
        return tables[name][1]

    sides = work_ref.shape[1]
    owned = sides // 2
    tiles = jnp.concatenate(read_slots(arrived_ref, capacity, window), axis=1)
    high, low = halves(tiles)
    taken = dot(ready("taker")[...], jnp.concatenate([high, low], axis=0))
    centre = ready("centre")[...]
    near_ref = ready("near")
    for c in range(6):
        values = taken[:, c * points : (c + 1) * points]
        work_ref[c] = (
            near_ref[0] * lane_gather(values, centre)
            + near_ref[1] * lane_gather(values, centre + 1)
            + near_ref[2] * lane_gather(values, (centre + 2) & (points - 1))
        )

    penalty_ref = ready("penalty")
    frame_ref = ready("frame")
    for b in range(2):
        ahead = [work_ref[3 * b + c, pl.ds(0, owned, stride=2), :] for c in range(3)]
        behind = [work_ref[3 * b + c, pl.ds(1, owned, stride=2), :] for c in range(3)]
        weight = penalty_ref[b]
        loads = [
            weight
            * (
                ahead[c]
                - (
                    frame_ref[3 * c] * behind[0]
                    + frame_ref[3 * c + 1] * behind[1]
                    + frame_ref[3 * c + 2] * behind[2]
                )
            )
            for c in range(3)
        ]
        for c in range(3):
            work_ref[3 * b + c, pl.ds(0, owned, stride=2), :] = loads[c]
            work_ref[3 * b + c, pl.ds(1, owned, stride=2), :] = -(
                frame_ref[c] * loads[0]
                + frame_ref[3 + c] * loads[1]
                + frame_ref[6 + c] * loads[2]
            )

    opening = ready("opening")[...]
    spread_ref = ready("spread")
    forces = []
    for c in range(6):
        loads = work_ref[c]
        one = lane_gather(loads, opening & (points - 1))
        two = lane_gather(loads, (opening + 1) & (points - 1))
        force = spread_ref[0] * one + spread_ref[3] * two
        for d in range(1, 3):
            force = force + pltpu.roll(spread_ref[d] * one + spread_ref[3 + d] * two, d, 1)
        forces.append(force)
    high, low = halves(jnp.concatenate(forces, axis=1))
    given = dot(ready("giver")[...], jnp.concatenate([high, low], axis=0))
    tiles = [given[:, c * points : (c + 1) * points] for c in range(5)]
    last = given[:, 5 * points :]
    quarter = window // 4
    pieces = [pltpu.roll(last, window - quarter * at, 1) for at in range(4)]
    for at, tile in enumerate(fold_window(tiles, pieces, window)):
        out_ref[:, at * capacity : (at + 1) * capacity, :] = tile.reshape(owners, capacity, points)


def interior_kernel(cfg, coupling_ref, _, field_ref, table_ref, out_ref, *work):
    first, batch, points = cfg
    applied, mixed = work[:batch], work[batch:]

    def apply_left(b):
        high, low = halves(table_ref[b, 0:3].reshape(3 * points, points))
        parts = [halves(field_ref[b, c]) for c in range(6)]
        field_high = jnp.concatenate([part[0] for part in parts], axis=1)
        field_low = jnp.concatenate([part[1] for part in parts], axis=1)
        applied[b][...] = dot(
            jnp.concatenate([high, low], axis=1),
            jnp.concatenate([field_high, field_high], axis=0),
        ) + dot(high, field_low)

    def mix(b):
        patch = pl.program_id(0) * batch + b + first
        groups = (((0, 0), (3, 1), (4, 2)), ((1, 1),), ((2, 2),))
        for c in range(6):
            for g, terms in enumerate(groups):
                total = None
                for t, m in terms:
                    for d in range(6):
                        rows = slice(m * points, (m + 1) * points)
                        cols = slice(d * points, (d + 1) * points)
                        value = coupling_ref[patch, (t * 6 + c) * 6 + d] * applied[b][rows, cols]
                        total = value if total is None else total + value
                high, low = halves(total)
                rows = slice(c * points, (c + 1) * points)
                mixed[b][rows, g * points : (g + 1) * points] = high
                mixed[b][rows, (3 + g) * points : (4 + g) * points] = low

    def apply_right(b):
        high, low = halves(
            jnp.concatenate([table_ref[b, 4], table_ref[b, 3], table_ref[b, 5]], axis=1)
        )
        right = jnp.concatenate([high, low], axis=0)
        both = dot_nt(mixed[b][...], jnp.concatenate([right, right], axis=1))
        total = both[:, :points] + both[:, points:]
        out_ref[b] = total.reshape(6, points, points)

    apply_left(0)
    for b in range(batch):
        if b + 1 < batch:
            apply_left(b + 1)
        if b > 0:
            apply_right(b - 1)
        mix(b)
    apply_right(batch - 1)


def finish_kernel(
    cfg,
    gather_ref,
    start_ref,
    arrived_ref,
    first_ref,
    second_ref,
    out_ref,
    held_ref,
    edge_ref,
    turned_ref,
    arrival,
    leaving,
):
    per_device, capacity, window, batch, points = cfg
    edges = EDGES * per_device
    steps = per_device // batch
    half = steps // 2
    loads, stores = [], []
    for step in range(steps):
        source = first_ref if step < half else second_ref
        block = pl.ds(step % half * batch, batch)
        own = held_ref.at[pl.ds(step * batch, batch)]
        loads.append(pltpu.make_async_copy(source.at[block], own, arrival.at[step]))
        loads[-1].start()
        stores.append(
            pltpu.make_async_copy(own, out_ref.at[pl.ds(step * batch, batch)], leaving.at[step])
        )

    at = iota(start_ref.shape, 1) - start_ref[...] + 1
    valid = (at >= 0) & (at < window)
    index = at & (points - 1)
    tiles = [
        jnp.where(valid, lane_gather(tile, index), 0.0)
        for tile in read_slots(arrived_ref, capacity, window)
    ]
    high, low = halves(jnp.concatenate(tiles, axis=1))
    total = dot(gather_ref[...], jnp.concatenate([high, low], axis=0))
    for c in range(6):
        part = total[:, c * points : (c + 1) * points]
        edge_ref[c] = part
        high = part.astype(BF16).astype(F32)
        both = jnp.concatenate([high, part - high], axis=0)
        turned_ref[c * points : (c + 1) * points, :] = jnp.transpose(both).astype(BF16)

    width = batch * points
    kk = iota((2 * edges, width), 0) % edges
    at = iota((2 * edges, width), 1)
    lane = at % points
    which = kk % EDGES
    near = lane == jnp.where(which == 1, points - 1, jnp.where(which == 2, 0, -1))
    next_to = lane == jnp.where(which == 1, points - 2, jnp.where(which == 2, 1, -1))
    weight = jnp.where(near, 1.5, jnp.where(next_to, -0.5, 0.0))
    ahead = kk // EDGES - at // points
    sub = iota((ROWS, points), 0)
    for step in range(steps):
        select = jnp.where(ahead == step * batch, weight, 0.0).astype(BF16)
        add = dot(turned_ref[...], select)
        loads[step].wait()
        for b in range(batch):
            patch = step * batch + b
            for c in range(6):
                value = held_ref[patch, c]
                value = value + add[c * points : (c + 1) * points, b * points : (b + 1) * points]
                top = edge_ref[c, EDGES * patch : EDGES * patch + 1, :]
                bottom = edge_ref[c, EDGES * patch + 3 : EDGES * patch + 4, :]
                held_ref[patch, c, 0:ROWS] = value[0:ROWS] + jnp.where(
                    sub == 0, 1.5 * top, jnp.where(sub == 1, -0.5 * top, 0.0)
                )
                held_ref[patch, c, ROWS : points - ROWS] = value[ROWS : points - ROWS]
                held_ref[patch, c, points - ROWS :] = value[points - ROWS :] + jnp.where(
                    sub == ROWS - 1, 1.5 * bottom, jnp.where(sub == ROWS - 2, -0.5 * bottom, 0.0)
                )
        stores[step].start()
    for store in stores:
        store.wait()


def exchange(payload):
    return lax.all_to_all(payload, ("chip", "cores"), split_axis=0, concat_axis=0, tiled=True)


def whole(shape):
    return pl.BlockSpec(shape, lambda *_: (0,) * len(shape))


def in_hbm(value):
    return pltpu.with_memory_space_constraint(value, pltpu.HBM)


def params(mib):
    return pltpu.CompilerParams(vmem_limit_bytes=mib * MIB)


def shards(patch_field, patch_tables, coupling, side_device, side_detail, penalty, angles):
    devices = lax.axis_size(("chip", "cores"))
    me = lax.axis_index(("chip", "cores")).astype(I32).reshape(1)
    per_device, _, points, _ = patch_field.shape
    owned = penalty.shape[0]
    sides = 2 * owned
    capacity = -(-max(2, 2 * sides // devices) // ROWS) * ROWS
    slots = devices * capacity
    edges = EDGES * per_device
    window = 3 * points // 4 + 4
    fields = Codes(per_device, points)
    smem = pl.BlockSpec(memory_space=pltpu.SMEM)
    vmem = pl.BlockSpec(memory_space=pltpu.VMEM)
    patch_field, patch_tables = in_hbm(patch_field), in_hbm(patch_tables)
    device_row = side_device.reshape(1, -1)
    detail_rows = side_detail.T
    payload_shape = (devices, 5 * capacity, points)
    payload = pltpu.HBM(payload_shape, F32)
    coupling = coupling.reshape(per_device, -1)
    weights = in_hbm(jnp.swapaxes(penalty, 0, 1))

    batch = 4
    outgoing = pl.pallas_call(
        functools.partial(
            pack_kernel, (fields, devices, per_device, capacity, window, batch, points)
        ),
        name="pack",
        out_shape=payload,
        grid=(1,),
        in_specs=[
            smem,
            whole(device_row.shape),
            whole(detail_rows.shape),
            pl.BlockSpec(memory_space=pl.ANY),
        ],
        out_specs=whole(payload_shape),
        scratch_shapes=[
            pltpu.VMEM(patch_field.shape, F32),
            pltpu.VMEM((6, edges, points), F32),
            pltpu.SemaphoreType.DMA((per_device,)),
        ],
        compiler_params=params(56),
    )(me, device_row, detail_rows, patch_field)
    arrived = exchange(outgoing)

    def tied(value, after):
        return lax.optimization_barrier((value, after))[0]

    def table(shape, kind):
        return pltpu.HBM(shape, kind)

    tables = pl.pallas_call(
        functools.partial(tables_kernel, (fields, devices, per_device, capacity, points)),
        name="tables",
        out_shape=[
            table((edges, 2 * slots), BF16),
            table((slots, points), I32),
            table((sides, 2 * slots), BF16),
            table((slots, 2 * sides), BF16),
            table((sides, points), I32),
            table((3, sides, points), F32),
            table((sides, points), I32),
            table((6, sides, points), F32),
            table((9, owned, points), F32),
        ],
        in_specs=[smem] + [vmem] * 3,
        out_specs=[vmem] * 9,
        compiler_params=params(56),
    )(tied(me, outgoing), device_row, detail_rows, angles.T)
    tables = [in_hbm(value) for value in tables]
    gather, start_table = tables[:2]

    def interior(begin, end, after):
        count = end - begin
        block = pl.BlockSpec((batch, 6, points, points), lambda i: (i + begin // batch, 0, 0, 0))
        shape = (count,) + patch_field.shape[1:]
        return pl.pallas_call(
            functools.partial(interior_kernel, (begin, batch, points)),
            name="interior",
            out_shape=pltpu.HBM(shape, F32) if begin else jax.ShapeDtypeStruct(shape, F32),
            grid=(count // batch,),
            in_specs=[smem, smem, block, block],
            out_specs=pl.BlockSpec((batch, 6, points, points), lambda i: (i, 0, 0, 0)),
            scratch_shapes=[pltpu.VMEM((3 * points, 6 * points), F32)] * batch
            + [pltpu.VMEM((6 * points, 6 * points), BF16)] * batch,
            compiler_params=params(52),
            cost_estimate=pl.CostEstimate(
                flops=count * 6 * 6 * 6 * points**3,
                bytes_accessed=count * 18 * points * points * 4,
                transcendentals=0,
            ),
        )(coupling, tied(me, after), patch_field, patch_tables)

    half = per_device // 2
    first = interior(0, half, outgoing)
    weights = tied(weights, first)
    taker, giver, centre, near, opening, spread, frame = tables[2:]
    held = (taker, centre, near, weights, frame, opening, spread, giver)
    back = pl.pallas_call(
        functools.partial(owner_kernel, (devices, capacity, window, points)),
        name="owner",
        out_shape=payload,
        in_specs=[vmem] + [pl.BlockSpec(memory_space=pl.ANY)] * 8,
        out_specs=vmem,
        scratch_shapes=[pltpu.VMEM((6, sides, points), F32)]
        + [pltpu.VMEM(t.shape, t.dtype) for t in held]
        + [pltpu.SemaphoreType.DMA((len(held),))],
        compiler_params=params(40),
    )(arrived, weights, *tables[2:])
    returned = exchange(back)
    second = in_hbm(interior(half, per_device, back))
    gather = tied(gather, second)

    batch = 2
    anywhere = pl.BlockSpec(memory_space=pl.ANY)
    return pl.pallas_call(
        functools.partial(finish_kernel, (per_device, capacity, window, batch, points)),
        name="finish",
        out_shape=jax.ShapeDtypeStruct(patch_field.shape, F32),
        grid=(1,),
        in_specs=[
            whole(gather.shape),
            whole(start_table.shape),
            vmem,
            anywhere,
            anywhere,
        ],
        out_specs=anywhere,
        scratch_shapes=[
            pltpu.VMEM(patch_field.shape, F32),
            pltpu.VMEM((6, edges, points), F32),
            pltpu.VMEM((6 * points, 2 * edges), BF16),
            pltpu.SemaphoreType.DMA((per_device // batch,)),
            pltpu.SemaphoreType.DMA((per_device // batch,)),
        ],
        compiler_params=params(40),
    )(gather, start_table, returned, first, second)


def solution(mesh):
    return jax.shard_map(
        shards,
        mesh=mesh,
        in_specs=(
            P(("chip", "cores"), None, None, None),
            P(("chip", "cores"), None, None, None),
            P(("chip", "cores"), None, None, None),
            P(),
            P(),
            P(("chip", "cores"), None, None),
            P(("chip", "cores"), None),
        ),
        out_specs=P(("chip", "cores"), None, None, None),
        check_vma=False,
    )
```

```python
import functools

import jax
import jax.numpy as jnp
from jax import lax
from jax.experimental import pallas as pl
from jax.experimental.pallas import tpu as pltpu
from jax.sharding import PartitionSpec as P

F32 = jnp.float32
BF16 = jnp.bfloat16
I32 = jnp.int32
EDGES = 4
LANES = 128
ROWS = 8
MIB = 1024 * 1024


def iota(shape, axis):
    return lax.broadcasted_iota(I32, shape, axis)


def halves(values):
    high = values.astype(BF16)
    low = (values - high.astype(F32)).astype(BF16)
    return high, low


def dot(left, right):
    return lax.dot_general(left, right, (((1,), (0,)), ((), ())), preferred_element_type=F32)


def dot_nt(left, right):
    return lax.dot_general(left, right, (((1,), (1,)), ((), ())), preferred_element_type=F32)


def lane_gather(values, index):
    return jnp.take_along_axis(values, index, axis=1)


class Codes:
    def __init__(self, per_device, points):
        self.bits = (points - 1).bit_length()
        self.local_bits = max(1, (per_device - 1).bit_length())
        self.mask = (1 << self.bits) - 1
        self.at_start = self.bits
        self.at_edge = 2 * self.bits
        self.at_local = self.at_edge + 2
        self.at_device = self.at_local + self.local_bits

    def pack(self, device, detail):
        return (
            (device << self.at_device)
            | (detail[0] << self.at_local)
            | (detail[1] << self.at_edge)
            | (detail[2] << self.at_start)
            | detail[3]
        )

    def length(self, code):
        return code & self.mask

    def start(self, code):
        return (code >> self.at_start) & self.mask

    def edge(self, code):
        return (code >> self.at_edge) & 3

    def local(self, code):
        return (code >> self.at_local) & ((1 << self.local_bits) - 1)

    def device(self, code):
        return code >> self.at_device


def side_codes(fields, device, detail):
    return fields.pack(device, [detail[i : i + 1, :] for i in range(4)])


def edge_row(fields, code):
    return fields.local(code) * EDGES + ((EDGES - fields.edge(code)) & (EDGES - 1))


def slot_tables(fields, code, me, owners, capacity):
    sides = code.shape[1] // owners
    slots = owners * capacity
    spread = jnp.concatenate(
        [
            jnp.broadcast_to(code[:, o * sides : (o + 1) * sides], (capacity, sides))
            for o in range(owners)
        ],
        axis=0,
    )
    mine = fields.device(spread) == me
    earlier = (iota((sides, sides), 0) < iota((sides, sides), 1)).astype(F32).astype(BF16)
    rank = dot(mine.astype(F32).astype(BF16), earlier).astype(I32)
    wanted = iota((slots, sides), 0) % capacity
    value = (fields.start(spread) << 16) | (edge_row(fields, spread) + 1)
    chosen = jnp.where(mine & (rank == wanted), value.astype(F32), 0.0)
    found = jnp.sum(chosen, axis=1, keepdims=True).astype(I32)
    return (found & 0xFFFF) - 1, found >> 16


def fold_window(tiles, last_pieces, window):
    lane = iota(tiles[0].shape, 1)
    out = []
    for at in range(5):
        if at < 4:
            out.append(jnp.where(lane < window, tiles[at], last_pieces[at]))
        else:
            out.append(tiles[at])
    return out


def unfold_last(tiles, window):
    quarter = window // 4
    lane = iota(tiles[0].shape, 1)
    lanes = tiles[0].shape[1]
    value = None
    for at in range(4):
        shift = (lanes - (window - quarter * at)) % lanes
        piece = pltpu.roll(tiles[at], shift, 1)
        value = piece if value is None else jnp.where(lane >= quarter * at, piece, value)
    return value


def pack_kernel(
    cfg,
    me_ref,
    device_ref,
    detail_ref,
    field_ref,
    out_ref,
    held_ref,
    strips_ref,
    staged_ref,
    arrival,
    leaving,
):
    fields, owners, per_device, capacity, window, batch, points = cfg
    edges = EDGES * per_device
    slots = owners * capacity
    loads = []
    for patch in range(per_device):
        loads.append(
            pltpu.make_async_copy(field_ref.at[patch], held_ref.at[patch], arrival.at[patch])
        )
        loads[-1].start()

    code = side_codes(fields, device_ref[...], detail_ref)
    row, start = slot_tables(fields, code, me_ref[0], owners, capacity)
    picker = jnp.where(iota((slots, 2 * edges), 1) % edges == row, 1.0, 0.0).astype(BF16)
    base = iota((slots, points), 1) + start - 1

    lane = iota((points, points), 1)
    lane_of = iota((1, ROWS, points), 2)
    rows = EDGES * batch
    sub = iota((rows, points), 0)
    for step in range(per_device // batch):
        columns = jnp.zeros((points // ROWS, ROWS, points), F32)
        for b in range(batch):
            patch = step * batch + b
            loads[patch].wait()
            for c in range(6):
                at = EDGES * (c * batch + b)
                moved = pltpu.roll(held_ref[patch, c], (2 + at) % points, 1)
                moved = moved.reshape(columns.shape)
                hit = jnp.broadcast_to(lane_of // EDGES == at // EDGES, columns.shape)
                columns = jnp.where(hit, moved, columns)
        columns = columns.reshape(points, points)
        other = jnp.where(
            lane % EDGES == 1, pltpu.roll(columns, 1, 1), pltpu.roll(columns, points - 1, 1)
        )
        turned = jnp.transpose(1.5 * columns - 0.5 * other)
        for c in range(6):
            block = turned[c * rows : (c + 1) * rows]
            for b in range(batch):
                patch = step * batch + b
                top = 1.5 * held_ref[patch, c, 0:1, :] - 0.5 * held_ref[patch, c, 1:2, :]
                bottom = (
                    1.5 * held_ref[patch, c, points - 1 : points, :]
                    - 0.5 * held_ref[patch, c, points - 2 : points - 1, :]
                )
                block = jnp.where(sub == EDGES * b, top, block)
                block = jnp.where(sub == EDGES * b + 3, bottom, block)
            strips_ref[c, step * rows : (step + 1) * rows, :] = block

    high, low = halves(jnp.concatenate([strips_ref[c] for c in range(6)], axis=1))
    picked = dot(picker, jnp.concatenate([high, low], axis=0))
    quarter = window // 4
    tiles = [
        lane_gather(picked[:, c * points : (c + 1) * points], base & (points - 1))
        for c in range(5)
    ]
    last = lane_gather(picked[:, 5 * points :], base & (points - 1))
    pieces = [pltpu.roll(last, window - quarter * at, 1) for at in range(4)]
    copies = []
    for at, tile in enumerate(fold_window(tiles, pieces, window)):
        part = pl.ds(at * capacity, capacity)
        staged_ref[:, part, :] = tile.reshape(owners, capacity, points)
        copies.append(
            pltpu.make_async_copy(staged_ref.at[:, part], out_ref.at[:, part], leaving.at[at])
        )
        copies[-1].start()
    for copy in copies:
        copy.wait()


def read_slots(ref, capacity, window):
    owners, rows, lanes = ref.shape
    tiles = [
        ref[:, at * capacity : (at + 1) * capacity, :].reshape(owners * capacity, lanes)
        for at in range(5)
    ]
    tiles.append(unfold_last(tiles, window))
    return tiles


def tables_kernel(
    cfg,
    me_ref,
    device_ref,
    detail_ref,
    angle_ref,
    gather_ref,
    start_ref,
    taker_ref,
    giver_ref,
    centre_ref,
    near_ref,
    opening_ref,
    spread_ref,
    frame_ref,
):
    fields, owners, per_device, capacity, points = cfg
    edges = EDGES * per_device
    slots = owners * capacity
    sides = device_ref.shape[1] // owners
    owned = sides // 2
    me = me_ref[0]
    code = side_codes(fields, device_ref[...], detail_ref)
    row, start = slot_tables(fields, code, me, owners, capacity)
    picker = jnp.where(iota((slots, 2 * edges), 1) % edges == row, 1.0, 0.0)
    gather = jnp.transpose(picker)[:edges].astype(BF16)
    gather_ref[...] = jnp.concatenate([gather, gather], axis=1)
    start_ref[...] = jnp.broadcast_to(start, (slots, points))

    own = pl.ds(pl.multiple_of(me * sides, sides), sides)
    own_code = fields.pack(device_ref[:, own], [detail_ref[i : i + 1, own] for i in range(4)])
    code_row = jnp.broadcast_to(own_code, (sides, sides))
    code = jnp.transpose(code_row)
    device, device_row = fields.device(code), fields.device(code_row)
    same = device == device_row
    sub, lane = iota((sides, sides), 0), iota((sides, sides), 1)
    rank = jnp.sum(jnp.where(same & (lane < sub), 1.0, 0.0), axis=1, keepdims=True).astype(I32)
    rank_row = jnp.sum(jnp.where(same & (sub < lane), 1.0, 0.0), axis=0, keepdims=True).astype(I32)
    slot = device[:, 0:1] * capacity + rank
    slot_row = device_row[0:1] * capacity + rank_row
    taker_ref[...] = jnp.where(iota((sides, 2 * slots), 1) % slots == slot, 1.0, 0.0).astype(BF16)
    giver = jnp.where(iota((slots, sides), 0) == slot_row, 1.0, 0.0).astype(BF16)
    giver_ref[...] = jnp.concatenate([giver, giver], axis=1)

    start = fields.start(code)
    length = fields.length(code).astype(F32)
    quad = iota((sides, points), 1)
    param = (quad.astype(F32) + 0.5) * length * (1.0 / points)
    centre = (param + 0.5).astype(I32)
    offset = param - centre.astype(F32)
    centre_ref[...] = centre
    near_ref[0] = jnp.where(start + centre >= 1, 0.5 * jnp.square(0.5 - offset), 0.0)
    near_ref[1] = 0.75 - offset * offset
    near_ref[2] = jnp.where(start + centre + 1 < points, 0.5 * jnp.square(0.5 + offset), 0.0)
    opening = jnp.ceil((quad.astype(F32) - 0.5) * (float(points) / length) - 0.501).astype(I32)
    opening_ref[...] = opening
    for m in range(2):
        at = opening + m
        offset = (at.astype(F32) + 0.5) * length * (1.0 / points) - quad.astype(F32)
        inside = (at >= 0) & (at < points) & (offset >= -0.5) & (offset < 0.5)
        spread_ref[3 * m] = jnp.where(
            inside & (start + quad >= 1), 0.5 * jnp.square(0.5 - offset), 0.0
        )
        spread_ref[3 * m + 1] = jnp.where(inside, 0.75 - offset * offset, 0.0)
        spread_ref[3 * m + 2] = jnp.where(
            inside & (start + quad + 1 < points), 0.5 * jnp.square(0.5 + offset), 0.0
        )

    cosine, sine = jnp.cos(angle_ref[...]), jnp.sin(angle_ref[...])
    cos_a, cos_b, cos_g = [cosine[i : i + 1] for i in range(3)]
    sin_a, sin_b, sin_g = [sine[i : i + 1] for i in range(3)]
    entries = [
        cos_g * cos_b,
        cos_g * sin_b * sin_a - sin_g * cos_a,
        cos_g * sin_b * cos_a + sin_g * sin_a,
        sin_g * cos_b,
        sin_g * sin_b * sin_a + cos_g * cos_a,
        sin_g * sin_b * cos_a - cos_g * sin_a,
        -sin_b,
        cos_b * sin_a,
        cos_b * cos_a,
    ]
    for e, entry in enumerate(entries):
        frame_ref[e] = jnp.transpose(jnp.broadcast_to(entry, (points, owned)))


def owner_kernel(
    cfg,
    arrived_ref,
    penalty_ref,
    taker_ref,
    giver_ref,
    centre_ref,
    near_ref,
    opening_ref,
    spread_ref,
    frame_ref,
    out_ref,
    work_ref,
    *held,
):
    owners, capacity, window, points = cfg
    arrival = held[-1]
    tables = {}
    names = ("taker", "centre", "near", "penalty", "frame", "opening", "spread", "giver")
    sources = (
        taker_ref,
        centre_ref,
        near_ref,
        penalty_ref,
        frame_ref,
        opening_ref,
        spread_ref,
        giver_ref,
    )
    for at, (name, source) in enumerate(zip(names, sources)):
        tables[name] = (pltpu.make_async_copy(source, held[at], arrival.at[at]), held[at])
        tables[name][0].start()

    def ready(name):
        tables[name][0].wait()
        return tables[name][1]

    sides = work_ref.shape[1]
    owned = sides // 2
    tiles = jnp.concatenate(read_slots(arrived_ref, capacity, window), axis=1)
    high, low = halves(tiles)
    taken = dot(ready("taker")[...], jnp.concatenate([high, low], axis=0))
    centre = ready("centre")[...]
    near_ref = ready("near")
    for c in range(6):
        values = taken[:, c * points : (c + 1) * points]
        work_ref[c] = (
            near_ref[0] * lane_gather(values, centre)
            + near_ref[1] * lane_gather(values, centre + 1)
            + near_ref[2] * lane_gather(values, (centre + 2) & (points - 1))
        )

    penalty_ref = ready("penalty")
    frame_ref = ready("frame")
    for b in range(2):
        ahead = [work_ref[3 * b + c, pl.ds(0, owned, stride=2), :] for c in range(3)]
        behind = [work_ref[3 * b + c, pl.ds(1, owned, stride=2), :] for c in range(3)]
        weight = penalty_ref[b]
        loads = [
            weight
            * (
                ahead[c]
                - (
                    frame_ref[3 * c] * behind[0]
                    + frame_ref[3 * c + 1] * behind[1]
                    + frame_ref[3 * c + 2] * behind[2]
                )
            )
            for c in range(3)
        ]
        for c in range(3):
            work_ref[3 * b + c, pl.ds(0, owned, stride=2), :] = loads[c]
            work_ref[3 * b + c, pl.ds(1, owned, stride=2), :] = -(
                frame_ref[c] * loads[0]
                + frame_ref[3 + c] * loads[1]
                + frame_ref[6 + c] * loads[2]
            )

    opening = ready("opening")[...]
    spread_ref = ready("spread")
    forces = []
    for c in range(6):
        loads = work_ref[c]
        one = lane_gather(loads, opening & (points - 1))
        two = lane_gather(loads, (opening + 1) & (points - 1))
        force = spread_ref[0] * one + spread_ref[3] * two
        for d in range(1, 3):
            force = force + pltpu.roll(spread_ref[d] * one + spread_ref[3 + d] * two, d, 1)
        forces.append(force)
    high, low = halves(jnp.concatenate(forces, axis=1))
    given = dot(ready("giver")[...], jnp.concatenate([high, low], axis=0))
    tiles = [given[:, c * points : (c + 1) * points] for c in range(5)]
    last = given[:, 5 * points :]
    quarter = window // 4
    pieces = [pltpu.roll(last, window - quarter * at, 1) for at in range(4)]
    for at, tile in enumerate(fold_window(tiles, pieces, window)):
        out_ref[:, at * capacity : (at + 1) * capacity, :] = tile.reshape(owners, capacity, points)


def interior_kernel(cfg, coupling_ref, _, field_ref, table_ref, out_ref, *work):
    first, batch, points = cfg
    applied, mixed = work[:batch], work[batch:]

    def apply_left(b):
        high, low = halves(table_ref[b, 0:3].reshape(3 * points, points))
        parts = [halves(field_ref[b, c]) for c in range(6)]
        field_high = jnp.concatenate([part[0] for part in parts], axis=1)
        field_low = jnp.concatenate([part[1] for part in parts], axis=1)
        applied[b][...] = dot(
            jnp.concatenate([high, low], axis=1),
            jnp.concatenate([field_high, field_high], axis=0),
        ) + dot(high, field_low)

    def mix(b):
        patch = pl.program_id(0) * batch + b + first
        groups = (((0, 0), (3, 1), (4, 2)), ((1, 1),), ((2, 2),))
        for c in range(6):
            for g, terms in enumerate(groups):
                total = None
                for t, m in terms:
                    for d in range(6):
                        rows = slice(m * points, (m + 1) * points)
                        cols = slice(d * points, (d + 1) * points)
                        value = coupling_ref[patch, (t * 6 + c) * 6 + d] * applied[b][rows, cols]
                        total = value if total is None else total + value
                high, low = halves(total)
                rows = slice(c * points, (c + 1) * points)
                mixed[b][rows, g * points : (g + 1) * points] = high
                mixed[b][rows, (3 + g) * points : (4 + g) * points] = low

    def apply_right(b):
        high, low = halves(
            jnp.concatenate([table_ref[b, 4], table_ref[b, 3], table_ref[b, 5]], axis=1)
        )
        right = jnp.concatenate([high, low], axis=0)
        both = dot_nt(mixed[b][...], jnp.concatenate([right, right], axis=1))
        total = both[:, :points] + both[:, points:]
        out_ref[b] = total.reshape(6, points, points)

    apply_left(0)
    for b in range(batch):
        if b + 1 < batch:
            apply_left(b + 1)
        if b > 0:
            apply_right(b - 1)
        mix(b)
    apply_right(batch - 1)


def finish_kernel(
    cfg,
    gather_ref,
    start_ref,
    arrived_ref,
    first_ref,
    second_ref,
    out_ref,
    held_ref,
    edge_ref,
    turned_ref,
    arrival,
    leaving,
):
    per_device, capacity, window, batch, points = cfg
    edges = EDGES * per_device
    steps = per_device // batch
    half = first_ref.shape[0]
    loads, stores = [], []
    for step in range(steps):
        own = held_ref.at[pl.ds(step * batch, batch)]
        if step * batch >= half:
            block = pl.ds(step * batch - half, batch)
            loads.append(pltpu.make_async_copy(second_ref.at[block], own, arrival.at[step]))
            loads[-1].start()
        else:
            loads.append(None)
        stores.append(
            pltpu.make_async_copy(own, out_ref.at[pl.ds(step * batch, batch)], leaving.at[step])
        )

    at = iota(start_ref.shape, 1) - start_ref[...] + 1
    valid = (at >= 0) & (at < window)
    index = at & (points - 1)
    tiles = [
        jnp.where(valid, lane_gather(tile, index), 0.0)
        for tile in read_slots(arrived_ref, capacity, window)
    ]
    high, low = halves(jnp.concatenate(tiles, axis=1))
    total = dot(gather_ref[...], jnp.concatenate([high, low], axis=0))
    for c in range(6):
        part = total[:, c * points : (c + 1) * points]
        edge_ref[c] = part
        high = part.astype(BF16).astype(F32)
        both = jnp.concatenate([high, part - high], axis=0)
        turned_ref[c * points : (c + 1) * points, :] = jnp.transpose(both).astype(BF16)

    width = batch * points
    kk = iota((2 * edges, width), 0) % edges
    at = iota((2 * edges, width), 1)
    lane = at % points
    which = kk % EDGES
    near = lane == jnp.where(which == 1, points - 1, jnp.where(which == 2, 0, -1))
    next_to = lane == jnp.where(which == 1, points - 2, jnp.where(which == 2, 1, -1))
    weight = jnp.where(near, 1.5, jnp.where(next_to, -0.5, 0.0))
    ahead = kk // EDGES - at // points
    sub = iota((ROWS, points), 0)
    for step in range(steps):
        select = jnp.where(ahead == step * batch, weight, 0.0).astype(BF16)
        add = dot(turned_ref[...], select)
        inner_ref = first_ref
        if loads[step] is not None:
            loads[step].wait()
            inner_ref = held_ref
        for b in range(batch):
            patch = step * batch + b
            for c in range(6):
                value = inner_ref[patch, c]
                value = value + add[c * points : (c + 1) * points, b * points : (b + 1) * points]
                top = edge_ref[c, EDGES * patch : EDGES * patch + 1, :]
                bottom = edge_ref[c, EDGES * patch + 3 : EDGES * patch + 4, :]
                held_ref[patch, c, 0:ROWS] = value[0:ROWS] + jnp.where(
                    sub == 0, 1.5 * top, jnp.where(sub == 1, -0.5 * top, 0.0)
                )
                held_ref[patch, c, ROWS : points - ROWS] = value[ROWS : points - ROWS]
                held_ref[patch, c, points - ROWS :] = value[points - ROWS :] + jnp.where(
                    sub == ROWS - 1, 1.5 * bottom, jnp.where(sub == ROWS - 2, -0.5 * bottom, 0.0)
                )
        stores[step].start()
    for store in stores:
        store.wait()


def exchange(payload):
    return lax.all_to_all(payload, ("chip", "cores"), split_axis=0, concat_axis=0, tiled=True)


def whole(shape):
    return pl.BlockSpec(shape, lambda *_: (0,) * len(shape))


def in_hbm(value):
    return pltpu.with_memory_space_constraint(value, pltpu.HBM)


def params(mib):
    return pltpu.CompilerParams(vmem_limit_bytes=mib * MIB)


def shards(patch_field, patch_tables, coupling, side_device, side_detail, penalty, angles):
    devices = lax.axis_size(("chip", "cores"))
    me = lax.axis_index(("chip", "cores")).astype(I32).reshape(1)
    per_device, _, points, _ = patch_field.shape
    owned = penalty.shape[0]
    sides = 2 * owned
    capacity = -(-max(2, 2 * sides // devices) // ROWS) * ROWS
    slots = devices * capacity
    edges = EDGES * per_device
    window = 3 * points // 4 + 4
    fields = Codes(per_device, points)
    smem = pl.BlockSpec(memory_space=pltpu.SMEM)
    vmem = pl.BlockSpec(memory_space=pltpu.VMEM)
    patch_field, patch_tables = in_hbm(patch_field), in_hbm(patch_tables)
    device_row = side_device.reshape(1, -1)
    detail_rows = side_detail.T
    payload_shape = (devices, 5 * capacity, points)
    payload = pltpu.HBM(payload_shape, F32)
    coupling = coupling.reshape(per_device, -1)
    weights = in_hbm(jnp.swapaxes(penalty, 0, 1))

    batch = 4
    outgoing = pl.pallas_call(
        functools.partial(
            pack_kernel, (fields, devices, per_device, capacity, window, batch, points)
        ),
        name="pack",
        out_shape=payload,
        grid=(1,),
        in_specs=[
            smem,
            whole(device_row.shape),
            whole(detail_rows.shape),
            pl.BlockSpec(memory_space=pl.ANY),
        ],
        out_specs=pl.BlockSpec(memory_space=pl.ANY),
        scratch_shapes=[
            pltpu.VMEM(patch_field.shape, F32),
            pltpu.VMEM((6, edges, points), F32),
            pltpu.VMEM(payload_shape, F32),
            pltpu.SemaphoreType.DMA((per_device,)),
            pltpu.SemaphoreType.DMA((5,)),
        ],
        compiler_params=params(56),
    )(me, device_row, detail_rows, patch_field)
    arrived = exchange(outgoing)

    def tied(value, after):
        return lax.optimization_barrier((value, after))[0]

    def table(shape, kind):
        return pltpu.HBM(shape, kind)

    tables = pl.pallas_call(
        functools.partial(tables_kernel, (fields, devices, per_device, capacity, points)),
        name="tables",
        out_shape=[
            table((edges, 2 * slots), BF16),
            table((slots, points), I32),
            table((sides, 2 * slots), BF16),
            table((slots, 2 * sides), BF16),
            table((sides, points), I32),
            table((3, sides, points), F32),
            table((sides, points), I32),
            table((6, sides, points), F32),
            table((9, owned, points), F32),
        ],
        in_specs=[smem] + [vmem] * 3,
        out_specs=[vmem] * 9,
        compiler_params=params(56),
    )(tied(me, outgoing), device_row, detail_rows, angles.T)
    tables = [in_hbm(value) for value in tables]
    gather, start_table = tables[:2]

    def interior(begin, end, after):
        count = end - begin
        block = pl.BlockSpec((batch, 6, points, points), lambda i: (i + begin // batch, 0, 0, 0))
        shape = (count,) + patch_field.shape[1:]
        return pl.pallas_call(
            functools.partial(interior_kernel, (begin, batch, points)),
            name="interior",
            out_shape=pltpu.HBM(shape, F32) if begin else jax.ShapeDtypeStruct(shape, F32),
            grid=(count // batch,),
            in_specs=[smem, smem, block, block],
            out_specs=pl.BlockSpec((batch, 6, points, points), lambda i: (i, 0, 0, 0)),
            scratch_shapes=[pltpu.VMEM((3 * points, 6 * points), F32)] * batch
            + [pltpu.VMEM((6 * points, 6 * points), BF16)] * batch,
            compiler_params=params(52),
            cost_estimate=pl.CostEstimate(
                flops=count * 6 * 6 * 6 * points**3,
                bytes_accessed=count * 18 * points * points * 4,
                transcendentals=0,
            ),
        )(coupling, tied(me, after), patch_field, patch_tables)

    half = per_device // 2
    first = interior(0, half, outgoing)
    weights = tied(weights, first)
    taker, giver, centre, near, opening, spread, frame = tables[2:]
    held = (taker, centre, near, weights, frame, opening, spread, giver)
    back = pl.pallas_call(
        functools.partial(owner_kernel, (devices, capacity, window, points)),
        name="owner",
        out_shape=payload,
        in_specs=[vmem] + [pl.BlockSpec(memory_space=pl.ANY)] * 8,
        out_specs=vmem,
        scratch_shapes=[pltpu.VMEM((6, sides, points), F32)]
        + [pltpu.VMEM(t.shape, t.dtype) for t in held]
        + [pltpu.SemaphoreType.DMA((len(held),))],
        compiler_params=params(40),
    )(arrived, weights, *tables[2:])
    returned = exchange(back)
    second = in_hbm(interior(half, per_device, back))
    gather = tied(gather, second)

    anywhere = pl.BlockSpec(memory_space=pl.ANY)
    return pl.pallas_call(
        functools.partial(finish_kernel, (per_device, capacity, window, batch, points)),
        name="finish",
        out_shape=jax.ShapeDtypeStruct(patch_field.shape, F32),
        grid=(1,),
        in_specs=[
            whole(gather.shape),
            whole(start_table.shape),
            vmem,
            vmem,
            anywhere,
        ],
        out_specs=anywhere,
        scratch_shapes=[
            pltpu.VMEM(patch_field.shape, F32),
            pltpu.VMEM((6, edges, points), F32),
            pltpu.VMEM((6 * points, 2 * edges), BF16),
            pltpu.SemaphoreType.DMA((per_device // batch,)),
            pltpu.SemaphoreType.DMA((per_device // batch,)),
        ],
        compiler_params=params(40),
    )(gather, start_table, returned, first, second)


def solution(mesh):
    return jax.shard_map(
        shards,
        mesh=mesh,
        in_specs=(
            P(("chip", "cores"), None, None, None),
            P(("chip", "cores"), None, None, None),
            P(("chip", "cores"), None, None, None),
            P(),
            P(),
            P(("chip", "cores"), None, None),
            P(("chip", "cores"), None),
        ),
        out_specs=P(("chip", "cores"), None, None, None),
        check_vma=False,
    )
```

```python
import functools

import jax
import jax.numpy as jnp
from jax import lax
from jax.experimental import pallas as pl
from jax.experimental.pallas import tpu as pltpu
from jax.sharding import PartitionSpec as P

F32 = jnp.float32
BF16 = jnp.bfloat16
I32 = jnp.int32
EDGES = 4
LANES = 128
ROWS = 8
MIB = 1024 * 1024


def iota(shape, axis):
    return lax.broadcasted_iota(I32, shape, axis)


def halves(values):
    high = values.astype(BF16)
    low = (values - high.astype(F32)).astype(BF16)
    return high, low


def dot(left, right):
    return lax.dot_general(left, right, (((1,), (0,)), ((), ())), preferred_element_type=F32)


def dot_nt(left, right):
    return lax.dot_general(left, right, (((1,), (1,)), ((), ())), preferred_element_type=F32)


def lane_gather(values, index):
    return jnp.take_along_axis(values, index, axis=1)


class Codes:
    def __init__(self, per_device, points):
        self.bits = (points - 1).bit_length()
        self.local_bits = max(1, (per_device - 1).bit_length())
        self.mask = (1 << self.bits) - 1
        self.at_start = self.bits
        self.at_edge = 2 * self.bits
        self.at_local = self.at_edge + 2
        self.at_device = self.at_local + self.local_bits

    def pack(self, device, detail):
        return (
            (device << self.at_device)
            | (detail[0] << self.at_local)
            | (detail[1] << self.at_edge)
            | (detail[2] << self.at_start)
            | detail[3]
        )

    def length(self, code):
        return code & self.mask

    def start(self, code):
        return (code >> self.at_start) & self.mask

    def edge(self, code):
        return (code >> self.at_edge) & 3

    def local(self, code):
        return (code >> self.at_local) & ((1 << self.local_bits) - 1)

    def device(self, code):
        return code >> self.at_device


def side_codes(fields, device, detail):
    return fields.pack(device, [detail[i : i + 1, :] for i in range(4)])


def edge_row(fields, code):
    return fields.local(code) * EDGES + ((EDGES - fields.edge(code)) & (EDGES - 1))


def slot_tables(fields, code, me, owners, capacity):
    sides = code.shape[1] // owners
    slots = owners * capacity
    spread = jnp.concatenate(
        [
            jnp.broadcast_to(code[:, o * sides : (o + 1) * sides], (capacity, sides))
            for o in range(owners)
        ],
        axis=0,
    )
    mine = fields.device(spread) == me
    earlier = (iota((sides, sides), 0) < iota((sides, sides), 1)).astype(F32).astype(BF16)
    rank = dot(mine.astype(F32).astype(BF16), earlier).astype(I32)
    wanted = iota((slots, sides), 0) % capacity
    value = (fields.start(spread) << 16) | (edge_row(fields, spread) + 1)
    chosen = jnp.where(mine & (rank == wanted), value.astype(F32), 0.0)
    found = jnp.sum(chosen, axis=1, keepdims=True).astype(I32)
    return (found & 0xFFFF) - 1, found >> 16


def fold_window(tiles, last_pieces, window):
    lane = iota(tiles[0].shape, 1)
    out = []
    for at in range(5):
        if at < 4:
            out.append(jnp.where(lane < window, tiles[at], last_pieces[at]))
        else:
            out.append(tiles[at])
    return out


def unfold_last(tiles, window):
    quarter = window // 4
    lane = iota(tiles[0].shape, 1)
    lanes = tiles[0].shape[1]
    value = None
    for at in range(4):
        shift = (lanes - (window - quarter * at)) % lanes
        piece = pltpu.roll(tiles[at], shift, 1)
        value = piece if value is None else jnp.where(lane >= quarter * at, piece, value)
    return value


def pack_kernel(
    cfg,
    me_ref,
    device_ref,
    detail_ref,
    field_ref,
    out_ref,
    held_ref,
    strips_ref,
    staged_ref,
    arrival,
    leaving,
):
    fields, owners, per_device, capacity, window, batch, points = cfg
    edges = EDGES * per_device
    slots = owners * capacity
    loads = []
    for patch in range(per_device):
        loads.append(
            pltpu.make_async_copy(field_ref.at[patch], held_ref.at[patch], arrival.at[patch])
        )
        loads[-1].start()

    code = side_codes(fields, device_ref[...], detail_ref)
    row, start = slot_tables(fields, code, me_ref[0], owners, capacity)
    picker = jnp.where(iota((slots, 2 * edges), 1) % edges == row, 1.0, 0.0).astype(BF16)
    base = iota((slots, points), 1) + start - 1

    lane = iota((points, points), 1)
    lane_of = iota((1, ROWS, points), 2)
    rows = EDGES * batch
    sub = iota((rows, points), 0)
    for step in range(per_device // batch):
        columns = jnp.zeros((points // ROWS, ROWS, points), F32)
        for b in range(batch):
            patch = step * batch + b
            loads[patch].wait()
            for c in range(6):
                at = EDGES * (c * batch + b)
                moved = pltpu.roll(held_ref[patch, c], (2 + at) % points, 1)
                moved = moved.reshape(columns.shape)
                hit = jnp.broadcast_to(lane_of // EDGES == at // EDGES, columns.shape)
                columns = jnp.where(hit, moved, columns)
        columns = columns.reshape(points, points)
        other = jnp.where(
            lane % EDGES == 1, pltpu.roll(columns, 1, 1), pltpu.roll(columns, points - 1, 1)
        )
        turned = jnp.transpose(1.5 * columns - 0.5 * other)
        for c in range(6):
            block = turned[c * rows : (c + 1) * rows]
            for b in range(batch):
                patch = step * batch + b
                top = 1.5 * held_ref[patch, c, 0:1, :] - 0.5 * held_ref[patch, c, 1:2, :]
                bottom = (
                    1.5 * held_ref[patch, c, points - 1 : points, :]
                    - 0.5 * held_ref[patch, c, points - 2 : points - 1, :]
                )
                block = jnp.where(sub == EDGES * b, top, block)
                block = jnp.where(sub == EDGES * b + 3, bottom, block)
            strips_ref[c, step * rows : (step + 1) * rows, :] = block

    high, low = halves(jnp.concatenate([strips_ref[c] for c in range(6)], axis=1))
    picked = dot(picker, jnp.concatenate([high, low], axis=0))
    quarter = window // 4
    tiles = [
        lane_gather(picked[:, c * points : (c + 1) * points], base & (points - 1))
        for c in range(5)
    ]
    last = lane_gather(picked[:, 5 * points :], base & (points - 1))
    pieces = [pltpu.roll(last, window - quarter * at, 1) for at in range(4)]
    copies = []
    for at, tile in enumerate(fold_window(tiles, pieces, window)):
        part = pl.ds(at * capacity, capacity)
        staged_ref[:, part, :] = tile.reshape(owners, capacity, points)
        copies.append(
            pltpu.make_async_copy(staged_ref.at[:, part], out_ref.at[:, part], leaving.at[at])
        )
        copies[-1].start()
    for copy in copies:
        copy.wait()


def read_slots(ref, capacity, window):
    owners, rows, lanes = ref.shape
    tiles = [
        ref[:, at * capacity : (at + 1) * capacity, :].reshape(owners * capacity, lanes)
        for at in range(5)
    ]
    tiles.append(unfold_last(tiles, window))
    return tiles


def slots_kernel(cfg, me_ref, device_ref, detail_ref, gather_ref, start_ref):
    fields, owners, per_device, capacity, points = cfg
    edges = EDGES * per_device
    slots = owners * capacity
    code = side_codes(fields, device_ref[...], detail_ref)
    row, start = slot_tables(fields, code, me_ref[0], owners, capacity)
    picker = jnp.where(iota((slots, 2 * edges), 1) % edges == row, 1.0, 0.0)
    gather = jnp.transpose(picker)[:edges].astype(BF16)
    gather_ref[...] = jnp.concatenate([gather, gather], axis=1)
    start_ref[...] = jnp.broadcast_to(start, (slots, points))


def tables_kernel(
    cfg,
    me_ref,
    device_ref,
    detail_ref,
    angle_ref,
    taker_ref,
    giver_ref,
    centre_ref,
    near_ref,
    opening_ref,
    spread_ref,
    frame_ref,
):
    fields, owners, per_device, capacity, points = cfg
    slots = owners * capacity
    sides = device_ref.shape[1] // owners
    owned = sides // 2
    me = me_ref[0]
    own = pl.ds(pl.multiple_of(me * sides, sides), sides)
    own_code = fields.pack(device_ref[:, own], [detail_ref[i : i + 1, own] for i in range(4)])
    code_row = jnp.broadcast_to(own_code, (sides, sides))
    code = jnp.transpose(code_row)
    device, device_row = fields.device(code), fields.device(code_row)
    same = device == device_row
    sub, lane = iota((sides, sides), 0), iota((sides, sides), 1)
    rank = jnp.sum(jnp.where(same & (lane < sub), 1.0, 0.0), axis=1, keepdims=True).astype(I32)
    rank_row = jnp.sum(jnp.where(same & (sub < lane), 1.0, 0.0), axis=0, keepdims=True).astype(I32)
    slot = device[:, 0:1] * capacity + rank
    slot_row = device_row[0:1] * capacity + rank_row
    taker_ref[...] = jnp.where(iota((sides, 2 * slots), 1) % slots == slot, 1.0, 0.0).astype(BF16)
    giver = jnp.where(iota((slots, sides), 0) == slot_row, 1.0, 0.0).astype(BF16)
    giver_ref[...] = jnp.concatenate([giver, giver], axis=1)

    start = fields.start(code)
    length = fields.length(code).astype(F32)
    quad = iota((sides, points), 1)
    param = (quad.astype(F32) + 0.5) * length * (1.0 / points)
    centre = (param + 0.5).astype(I32)
    offset = param - centre.astype(F32)
    centre_ref[...] = centre
    near_ref[0] = jnp.where(start + centre >= 1, 0.5 * jnp.square(0.5 - offset), 0.0)
    near_ref[1] = 0.75 - offset * offset
    near_ref[2] = jnp.where(start + centre + 1 < points, 0.5 * jnp.square(0.5 + offset), 0.0)
    opening = jnp.ceil((quad.astype(F32) - 0.5) * (float(points) / length) - 0.501).astype(I32)
    opening_ref[...] = opening
    for m in range(2):
        at = opening + m
        offset = (at.astype(F32) + 0.5) * length * (1.0 / points) - quad.astype(F32)
        inside = (at >= 0) & (at < points) & (offset >= -0.5) & (offset < 0.5)
        spread_ref[3 * m] = jnp.where(
            inside & (start + quad >= 1), 0.5 * jnp.square(0.5 - offset), 0.0
        )
        spread_ref[3 * m + 1] = jnp.where(inside, 0.75 - offset * offset, 0.0)
        spread_ref[3 * m + 2] = jnp.where(
            inside & (start + quad + 1 < points), 0.5 * jnp.square(0.5 + offset), 0.0
        )

    cosine, sine = jnp.cos(angle_ref[...]), jnp.sin(angle_ref[...])
    cos_a, cos_b, cos_g = [cosine[i : i + 1] for i in range(3)]
    sin_a, sin_b, sin_g = [sine[i : i + 1] for i in range(3)]
    entries = [
        cos_g * cos_b,
        cos_g * sin_b * sin_a - sin_g * cos_a,
        cos_g * sin_b * cos_a + sin_g * sin_a,
        sin_g * cos_b,
        sin_g * sin_b * sin_a + cos_g * cos_a,
        sin_g * sin_b * cos_a - cos_g * sin_a,
        -sin_b,
        cos_b * sin_a,
        cos_b * cos_a,
    ]
    for e, entry in enumerate(entries):
        frame_ref[e] = jnp.transpose(jnp.broadcast_to(entry, (points, owned)))


def owner_kernel(
    cfg,
    arrived_ref,
    penalty_ref,
    taker_ref,
    giver_ref,
    centre_ref,
    near_ref,
    opening_ref,
    spread_ref,
    frame_ref,
    out_ref,
    work_ref,
    *held,
):
    owners, capacity, window, points = cfg
    arrival = held[-1]
    tables = {}
    names = ("taker", "centre", "near", "penalty", "frame", "opening", "spread", "giver")
    sources = (
        taker_ref,
        centre_ref,
        near_ref,
        penalty_ref,
        frame_ref,
        opening_ref,
        spread_ref,
        giver_ref,
    )
    for at, (name, source) in enumerate(zip(names, sources)):
        tables[name] = (pltpu.make_async_copy(source, held[at], arrival.at[at]), held[at])
        tables[name][0].start()

    def ready(name):
        tables[name][0].wait()
        return tables[name][1]

    sides = work_ref.shape[1]
    owned = sides // 2
    tiles = jnp.concatenate(read_slots(arrived_ref, capacity, window), axis=1)
    high, low = halves(tiles)
    taken = dot(ready("taker")[...], jnp.concatenate([high, low], axis=0))
    centre = ready("centre")[...]
    near_ref = ready("near")
    for c in range(6):
        values = taken[:, c * points : (c + 1) * points]
        work_ref[c] = (
            near_ref[0] * lane_gather(values, centre)
            + near_ref[1] * lane_gather(values, centre + 1)
            + near_ref[2] * lane_gather(values, (centre + 2) & (points - 1))
        )

    penalty_ref = ready("penalty")
    frame_ref = ready("frame")
    for b in range(2):
        ahead = [work_ref[3 * b + c, pl.ds(0, owned, stride=2), :] for c in range(3)]
        behind = [work_ref[3 * b + c, pl.ds(1, owned, stride=2), :] for c in range(3)]
        weight = penalty_ref[b]
        loads = [
            weight
            * (
                ahead[c]
                - (
                    frame_ref[3 * c] * behind[0]
                    + frame_ref[3 * c + 1] * behind[1]
                    + frame_ref[3 * c + 2] * behind[2]
                )
            )
            for c in range(3)
        ]
        for c in range(3):
            work_ref[3 * b + c, pl.ds(0, owned, stride=2), :] = loads[c]
            work_ref[3 * b + c, pl.ds(1, owned, stride=2), :] = -(
                frame_ref[c] * loads[0]
                + frame_ref[3 + c] * loads[1]
                + frame_ref[6 + c] * loads[2]
            )

    opening = ready("opening")[...]
    spread_ref = ready("spread")
    forces = []
    for c in range(6):
        loads = work_ref[c]
        one = lane_gather(loads, opening & (points - 1))
        two = lane_gather(loads, (opening + 1) & (points - 1))
        force = spread_ref[0] * one + spread_ref[3] * two
        for d in range(1, 3):
            force = force + pltpu.roll(spread_ref[d] * one + spread_ref[3 + d] * two, d, 1)
        forces.append(force)
    high, low = halves(jnp.concatenate(forces, axis=1))
    given = dot(ready("giver")[...], jnp.concatenate([high, low], axis=0))
    tiles = [given[:, c * points : (c + 1) * points] for c in range(5)]
    last = given[:, 5 * points :]
    quarter = window // 4
    pieces = [pltpu.roll(last, window - quarter * at, 1) for at in range(4)]
    for at, tile in enumerate(fold_window(tiles, pieces, window)):
        out_ref[:, at * capacity : (at + 1) * capacity, :] = tile.reshape(owners, capacity, points)


def interior_kernel(cfg, coupling_ref, _, field_ref, table_ref, out_ref, *work):
    first, batch, points = cfg
    applied, mixed = work[:batch], work[batch:]

    def apply_left(b):
        high, low = halves(table_ref[b, 0:3].reshape(3 * points, points))
        parts = [halves(field_ref[b, c]) for c in range(6)]
        field_high = jnp.concatenate([part[0] for part in parts], axis=1)
        field_low = jnp.concatenate([part[1] for part in parts], axis=1)
        applied[b][...] = dot(
            jnp.concatenate([high, low], axis=1),
            jnp.concatenate([field_high, field_high], axis=0),
        ) + dot(high, field_low)

    def mix(b):
        patch = pl.program_id(0) * batch + b + first
        groups = (((0, 0), (3, 1), (4, 2)), ((1, 1),), ((2, 2),))
        for c in range(6):
            for g, terms in enumerate(groups):
                total = None
                for t, m in terms:
                    for d in range(6):
                        rows = slice(m * points, (m + 1) * points)
                        cols = slice(d * points, (d + 1) * points)
                        value = coupling_ref[patch, (t * 6 + c) * 6 + d] * applied[b][rows, cols]
                        total = value if total is None else total + value
                high, low = halves(total)
                rows = slice(c * points, (c + 1) * points)
                mixed[b][rows, g * points : (g + 1) * points] = high
                mixed[b][rows, (3 + g) * points : (4 + g) * points] = low

    def apply_right(b):
        high, low = halves(
            jnp.concatenate([table_ref[b, 4], table_ref[b, 3], table_ref[b, 5]], axis=1)
        )
        right = jnp.concatenate([high, low], axis=0)
        both = dot_nt(mixed[b][...], jnp.concatenate([right, right], axis=1))
        total = both[:, :points] + both[:, points:]
        out_ref[b] = total.reshape(6, points, points)

    apply_left(0)
    for b in range(batch):
        if b + 1 < batch:
            apply_left(b + 1)
        if b > 0:
            apply_right(b - 1)
        mix(b)
    apply_right(batch - 1)


def finish_kernel(
    cfg,
    gather_ref,
    start_ref,
    arrived_ref,
    first_ref,
    second_ref,
    out_ref,
    held_ref,
    edge_ref,
    turned_ref,
    arrival,
    leaving,
):
    per_device, capacity, window, batch, points = cfg
    edges = EDGES * per_device
    steps = per_device // batch
    half = first_ref.shape[0]
    loads, stores = [], []
    for step in range(steps):
        own = held_ref.at[pl.ds(step * batch, batch)]
        if step * batch >= half:
            block = pl.ds(step * batch - half, batch)
            loads.append(pltpu.make_async_copy(second_ref.at[block], own, arrival.at[step]))
            loads[-1].start()
        else:
            loads.append(None)
        stores.append(
            pltpu.make_async_copy(own, out_ref.at[pl.ds(step * batch, batch)], leaving.at[step])
        )

    at = iota(start_ref.shape, 1) - start_ref[...] + 1
    valid = (at >= 0) & (at < window)
    index = at & (points - 1)
    tiles = [
        jnp.where(valid, lane_gather(tile, index), 0.0)
        for tile in read_slots(arrived_ref, capacity, window)
    ]
    high, low = halves(jnp.concatenate(tiles, axis=1))
    total = dot(gather_ref[...], jnp.concatenate([high, low], axis=0))
    for c in range(6):
        part = total[:, c * points : (c + 1) * points]
        edge_ref[c] = part
        high = part.astype(BF16).astype(F32)
        both = jnp.concatenate([high, part - high], axis=0)
        turned_ref[c * points : (c + 1) * points, :] = jnp.transpose(both).astype(BF16)

    width = batch * points
    kk = iota((2 * edges, width), 0) % edges
    at = iota((2 * edges, width), 1)
    lane = at % points
    which = kk % EDGES
    near = lane == jnp.where(which == 1, points - 1, jnp.where(which == 2, 0, -1))
    next_to = lane == jnp.where(which == 1, points - 2, jnp.where(which == 2, 1, -1))
    weight = jnp.where(near, 1.5, jnp.where(next_to, -0.5, 0.0))
    ahead = kk // EDGES - at // points
    sub = iota((ROWS, points), 0)
    for step in range(steps):
        select = jnp.where(ahead == step * batch, weight, 0.0).astype(BF16)
        add = dot(turned_ref[...], select)
        inner_ref = first_ref
        if loads[step] is not None:
            loads[step].wait()
            inner_ref = held_ref
        for b in range(batch):
            patch = step * batch + b
            for c in range(6):
                value = inner_ref[patch, c]
                value = value + add[c * points : (c + 1) * points, b * points : (b + 1) * points]
                top = edge_ref[c, EDGES * patch : EDGES * patch + 1, :]
                bottom = edge_ref[c, EDGES * patch + 3 : EDGES * patch + 4, :]
                held_ref[patch, c, 0:ROWS] = value[0:ROWS] + jnp.where(
                    sub == 0, 1.5 * top, jnp.where(sub == 1, -0.5 * top, 0.0)
                )
                held_ref[patch, c, ROWS : points - ROWS] = value[ROWS : points - ROWS]
                held_ref[patch, c, points - ROWS :] = value[points - ROWS :] + jnp.where(
                    sub == ROWS - 1, 1.5 * bottom, jnp.where(sub == ROWS - 2, -0.5 * bottom, 0.0)
                )
        stores[step].start()
    for store in stores:
        store.wait()


def exchange(payload):
    return lax.all_to_all(payload, ("chip", "cores"), split_axis=0, concat_axis=0, tiled=True)


def whole(shape):
    return pl.BlockSpec(shape, lambda *_: (0,) * len(shape))


def in_hbm(value):
    return pltpu.with_memory_space_constraint(value, pltpu.HBM)


def params(mib):
    return pltpu.CompilerParams(vmem_limit_bytes=mib * MIB)


def shards(patch_field, patch_tables, coupling, side_device, side_detail, penalty, angles):
    devices = lax.axis_size(("chip", "cores"))
    me = lax.axis_index(("chip", "cores")).astype(I32).reshape(1)
    per_device, _, points, _ = patch_field.shape
    owned = penalty.shape[0]
    sides = 2 * owned
    capacity = -(-max(2, 2 * sides // devices) // ROWS) * ROWS
    slots = devices * capacity
    edges = EDGES * per_device
    window = 3 * points // 4 + 4
    fields = Codes(per_device, points)
    smem = pl.BlockSpec(memory_space=pltpu.SMEM)
    vmem = pl.BlockSpec(memory_space=pltpu.VMEM)
    patch_field, patch_tables = in_hbm(patch_field), in_hbm(patch_tables)
    device_row = side_device.reshape(1, -1)
    detail_rows = side_detail.T
    payload_shape = (devices, 5 * capacity, points)
    payload = pltpu.HBM(payload_shape, F32)
    coupling = coupling.reshape(per_device, -1)
    weights = in_hbm(jnp.swapaxes(penalty, 0, 1))

    batch = 4
    outgoing = pl.pallas_call(
        functools.partial(
            pack_kernel, (fields, devices, per_device, capacity, window, batch, points)
        ),
        name="pack",
        out_shape=payload,
        grid=(1,),
        in_specs=[
            smem,
            whole(device_row.shape),
            whole(detail_rows.shape),
            pl.BlockSpec(memory_space=pl.ANY),
        ],
        out_specs=pl.BlockSpec(memory_space=pl.ANY),
        scratch_shapes=[
            pltpu.VMEM(patch_field.shape, F32),
            pltpu.VMEM((6, edges, points), F32),
            pltpu.VMEM(payload_shape, F32),
            pltpu.SemaphoreType.DMA((per_device,)),
            pltpu.SemaphoreType.DMA((5,)),
        ],
        compiler_params=params(56),
    )(me, device_row, detail_rows, patch_field)
    arrived = exchange(outgoing)

    def tied(value, after):
        return lax.optimization_barrier((value, after))[0]

    def table(shape, kind):
        return pltpu.HBM(shape, kind)

    tables = pl.pallas_call(
        functools.partial(tables_kernel, (fields, devices, per_device, capacity, points)),
        name="tables",
        out_shape=[
            table((sides, 2 * slots), BF16),
            table((slots, 2 * sides), BF16),
            table((sides, points), I32),
            table((3, sides, points), F32),
            table((sides, points), I32),
            table((6, sides, points), F32),
            table((9, owned, points), F32),
        ],
        in_specs=[smem] + [vmem] * 3,
        out_specs=[vmem] * 7,
        compiler_params=params(56),
    )(tied(me, outgoing), device_row, detail_rows, angles.T)
    tables = [in_hbm(value) for value in tables]

    def interior(begin, end, after):
        count = end - begin
        block = pl.BlockSpec((batch, 6, points, points), lambda i: (i + begin // batch, 0, 0, 0))
        shape = (count,) + patch_field.shape[1:]
        return pl.pallas_call(
            functools.partial(interior_kernel, (begin, batch, points)),
            name="interior",
            out_shape=pltpu.HBM(shape, F32) if begin else jax.ShapeDtypeStruct(shape, F32),
            grid=(count // batch,),
            in_specs=[smem, smem, block, block],
            out_specs=pl.BlockSpec((batch, 6, points, points), lambda i: (i, 0, 0, 0)),
            scratch_shapes=[pltpu.VMEM((3 * points, 6 * points), F32)] * batch
            + [pltpu.VMEM((6 * points, 6 * points), BF16)] * batch,
            compiler_params=params(52),
            cost_estimate=pl.CostEstimate(
                flops=count * 6 * 6 * 6 * points**3,
                bytes_accessed=count * 18 * points * points * 4,
                transcendentals=0,
            ),
        )(coupling, tied(me, after), patch_field, patch_tables)

    half = per_device // 2
    first = interior(0, half, outgoing)
    weights = tied(weights, first)
    taker, giver, centre, near, opening, spread, frame = tables
    held = (taker, centre, near, weights, frame, opening, spread, giver)
    back = pl.pallas_call(
        functools.partial(owner_kernel, (devices, capacity, window, points)),
        name="owner",
        out_shape=payload,
        in_specs=[vmem] + [pl.BlockSpec(memory_space=pl.ANY)] * 8,
        out_specs=vmem,
        scratch_shapes=[pltpu.VMEM((6, sides, points), F32)]
        + [pltpu.VMEM(t.shape, t.dtype) for t in held]
        + [pltpu.SemaphoreType.DMA((len(held),))],
        compiler_params=params(40),
    )(arrived, weights, *tables)
    returned = exchange(back)
    second = in_hbm(interior(half, per_device, back))
    gather, start_table = pl.pallas_call(
        functools.partial(slots_kernel, (fields, devices, per_device, capacity, points)),
        name="slots",
        out_shape=[table((edges, 2 * slots), BF16), table((slots, points), I32)],
        in_specs=[smem] + [vmem] * 2,
        out_specs=[vmem] * 2,
        compiler_params=params(56),
    )(tied(me, back), device_row, detail_rows)
    gather = in_hbm(tied(gather, second))
    start_table = in_hbm(start_table)

    anywhere = pl.BlockSpec(memory_space=pl.ANY)
    return pl.pallas_call(
        functools.partial(finish_kernel, (per_device, capacity, window, batch, points)),
        name="finish",
        out_shape=jax.ShapeDtypeStruct(patch_field.shape, F32),
        grid=(1,),
        in_specs=[
            whole(gather.shape),
            whole(start_table.shape),
            vmem,
            vmem,
            anywhere,
        ],
        out_specs=anywhere,
        scratch_shapes=[
            pltpu.VMEM(patch_field.shape, F32),
            pltpu.VMEM((6, edges, points), F32),
            pltpu.VMEM((6 * points, 2 * edges), BF16),
            pltpu.SemaphoreType.DMA((per_device // batch,)),
            pltpu.SemaphoreType.DMA((per_device // batch,)),
        ],
        compiler_params=params(40),
    )(gather, start_table, returned, first, second)


def solution(mesh):
    return jax.shard_map(
        shards,
        mesh=mesh,
        in_specs=(
            P(("chip", "cores"), None, None, None),
            P(("chip", "cores"), None, None, None),
            P(("chip", "cores"), None, None, None),
            P(),
            P(),
            P(("chip", "cores"), None, None),
            P(("chip", "cores"), None),
        ),
        out_specs=P(("chip", "cores"), None, None, None),
        check_vma=False,
    )
```
